768 devices in a mesh: gx: 96 (over x, z, core), gy: 8 (over y).
Axes of the slice: x: 4, y: 8, z: 12, core: 2. Of those that a mesh axis runs over, the one named last changes fastest.
Arguments:
- fields: bfloat16 [4, 6144, 1024], P(None, 'gx', 'gy'), may hold values from -6 to 6
- ocean_mask: int32 [6144, 1024], P('gx', 'gy'), may hold values from 0 to 1, as said below
- metric: float32 [2, 1024], P(None, 'gy'), may hold values from 1 to 4
- w_first: bfloat16 [5, 48, 4], replicated, may hold values from -1.5 to 1.5
- w_mid: bfloat16 [3, 5, 48, 48], replicated, may hold values from -0.4375 to 0.4375
- w_last: bfloat16 [5, 3, 48], replicated, may hold values from -0.4375 to 0.4375
- biases: float32 [4, 48], replicated, may hold values from -1.5 to 1.5
Outputs:
- forcing: float32 [2, 6144, 1024], P(None, 'gx', 'gy')
The draws below stay inside these ranges and needn't reach their ends.
Inputs may be any that keep to these rules, and one draw needn't show every extreme that they name: ocean_mask is constant on aligned blocks of 4 x 4 cells.
All inputs are finite; a program needn't handle non-finite values.
Results may differ from the reference program's by a relative error of at most 0.006.
The reference program's roundings to bfloat16 on the way count: a program that leaves them out, or rounds other values in their place, can miss the bound.
Values may be sent and summed in bfloat16 or wider, within the bound.
No kernel may reach another device: no remote copies, remote signals or barrier semaphores. Data moves between devices by JAX's collectives and lax.ppermute only.
A program may use at most 32 MiB of HBM per device.

```python
import math
import jax
import jax.numpy as jnp
from jax import lax

IN = 4
HID = 48
CX = 64
NX = 6144
NY = 1024


def draw_ocean_mask(key, part):
    coarse = jax.random.randint(key, (NX // 4, NY // 4), 0, 10)
    ocean = (coarse < 7).astype(jnp.int32)
    ocean = jnp.repeat(ocean, 4, axis=0)
    return jnp.repeat(ocean, 4, axis=1)


def steps_of(stream_key, dims, shards, least, largest):
    def one(axis_at, blocks):
        draws = jax.random.uniform(jax.random.fold_in(jax.random.fold_in(stream_key, 6), axis_at), (blocks,), jnp.float32, least / len(shards), largest / len(shards))
        return jnp.repeat(jnp.exp(draws), dims[axis_at] // blocks).reshape((-1,) + (1,) * (len(dims) - axis_at - 1))

    loudness = one(*shards[0])
    for cut in shards[1:]:
        loudness = loudness * one(*cut)
    return loudness


def bell_draw(rng, shape, deviation, limit, cuts=(), held_as=jnp.bfloat16):
    drawn = deviation * jax.random.normal(rng, shape, jnp.float32)
    if cuts:
        drawn = drawn * steps_of(rng, shape, cuts, -0.22, 0.18)
    return jnp.clip(drawn, -limit, limit).astype(held_as)


def setup_inputs(seed: int = 0) -> dict:
    key_list = jax.random.split(jax.random.key(seed), 8)
    return {
        "fields": bell_draw(key_list[0], (IN, NX, NY), 1.0, 6.0, ((1, 96), (2, 8))),
        "ocean_mask": draw_ocean_mask(jax.random.fold_in(key_list[7], 71), 0),
        "metric": jnp.clip(jnp.exp(math.log(4.0) - 1.3862944 * jax.random.uniform(key_list[2], (2, NY), jnp.float32) ** steps_of(key_list[2], (2, NY), ((1, 8),), -0.2, 0.2)), 1.0, 4.0),
        "w_first": bell_draw(key_list[3], (5, HID, IN), (9 * IN // 2) ** -0.5, 1.5),
        "w_mid": bell_draw(key_list[4], (3, 5, HID, HID), (9 * HID // 2) ** -0.5, 0.4375),
        "w_last": bell_draw(key_list[5], (5, 3, HID), (9 * HID // 2) ** -0.5, 0.4375),
        "biases": bell_draw(key_list[6], (4, HID), 0.3, 1.5, (), jnp.float32),
    }


pair_offsets = ((-1, -1), (-1, 0), (-1, 1), (0, -1))


def extend(values):
    cols_all = values.shape[1]
    rows_all = values.shape[2]
    widened = jnp.concatenate([values[:, -1:], values, values[:, :1]], axis=1)
    upper_rows = widened[:, ::-1, rows_all - 1:rows_all]
    below = jnp.zeros((values.shape[0], cols_all + 2, 1), values.dtype)
    return jnp.concatenate([below, widened, upper_rows], axis=2)


def stack_taps(padded):
    span_x = padded.shape[1] - 2
    span_y = padded.shape[2] - 2

    def part(shift_x, shift_y):
        return padded[:, 1 + shift_x:1 + shift_x + span_x, 1 + shift_y:1 + shift_y + span_y]

    stacked = [(part(step_x, step_y).astype(jnp.float32) + part(-step_x, -step_y).astype(jnp.float32)).astype(jnp.bfloat16) for step_x, step_y in pair_offsets]
    stacked.append(part(0, 0))
    return jnp.stack(stacked)


def conv_layer(values, weights, bias_row, ocean, rectify):
    padded = extend(values)

    def one_block(block_id):
        first_col = block_id * CX
        window = lax.dynamic_slice_in_dim(padded, first_col, CX + 2, 1)
        ocean_cols = lax.dynamic_slice_in_dim(ocean, first_col, CX, 0)
        tapped = stack_taps(window).astype(jnp.float32)
        summed = jnp.einsum("toc,tcxy->oxy", weights.astype(jnp.float32), tapped)
        summed = summed + bias_row[:, None, None]
        if rectify:
            summed = jax.nn.relu(summed)
        return (summed * ocean_cols[None]).astype(jnp.bfloat16)

    blocks = lax.map(one_block, jnp.arange(NX // CX, dtype=jnp.int32))
    return blocks.transpose(1, 0, 2, 3).reshape(blocks.shape[1], NX, NY)


def divergence(padded, metric, ocean):
    values = padded.astype(jnp.float32)
    half_inv_x = metric[0][None, :] * 0.5
    half_inv_y = metric[1][None, :] * 0.5

    def diff_x(plane):
        return (plane[2:, 1:-1] - plane[:-2, 1:-1]) * half_inv_x

    def diff_y(plane):
        return (plane[1:-1, 2:] - plane[1:-1, :-2]) * half_inv_y

    force_x = diff_x(values[0]) + diff_y(values[1])
    force_y = diff_x(values[1]) + diff_y(values[2])
    return jnp.stack([force_x, force_y]) * ocean[None]


def reference(fields, ocean_mask, metric, w_first, w_mid, w_last, biases):
    ocean = ocean_mask.astype(jnp.float32)
    hidden = conv_layer(fields, w_first, biases[0], ocean, True)
    for layer_id in range(3):
        hidden = conv_layer(hidden, w_mid[layer_id], biases[layer_id + 1], ocean, True)
    stress = conv_layer(hidden, w_last, jnp.zeros((3,), jnp.float32), ocean, False)
    return divergence(extend(stress), metric, ocean)
```

```python
import jax
import jax.numpy as jnp
from jax import lax
from jax.experimental import pallas as pl
from jax.experimental.pallas import tpu as pltpu
from jax.sharding import PartitionSpec as P

HALO = 8
BASE = 2 * HALO
UNROLL = 12
F32 = jnp.float32
BF16 = jnp.bfloat16


def iota(shape, dim):
    return lax.broadcasted_iota(jnp.int32, shape, dim)


def pack_kernel(flags, fields, mask, left, right, fwd, bwd):
    chans = fields.shape[0] + 1
    span_x, span_y = mask.shape
    wide = span_x + 2 * HALO
    lane = iota((wide, span_y), 1)
    low = jnp.zeros((wide, span_y), F32)
    top = jnp.zeros((wide, span_y), F32)
    for c in range(chans):
        own = fields[c].astype(F32) if c < chans - 1 else mask[...].astype(F32)
        col = jnp.concatenate([left[c].astype(F32), own, right[c].astype(F32)], axis=0)
        here = (lane >= c * HALO) & (lane < (c + 1) * HALO)
        low = jnp.where(here, pltpu.roll(col, c * HALO, 1) if c else col, low)
        top = jnp.where(here, pltpu.roll(col, (c + 1) * HALO, 1), top)
    fold = flags[1] == 1
    low = low.astype(BF16)
    top = top.astype(BF16)
    a, b = iota((span_y, span_y), 0), iota((span_y, span_y), 1)
    flip_y = ((a // HALO == b // HALO) & (a % HALO + b % HALO == HALO - 1)).astype(BF16)
    a, b = iota((wide, wide), 0), iota((wide, wide), 1)
    flip_x = (a + b == wide - 1).astype(BF16)
    turned = jnp.dot(top, flip_y, preferred_element_type=F32).astype(BF16)
    turned = jnp.dot(flip_x, turned, preferred_element_type=F32).astype(BF16)
    top = jnp.where(fold, turned, top)
    first = flags[0] == 1
    fwd[...] = jnp.where(first, top, low)
    bwd[...] = jnp.where(first, low, top)


def main_kernel(
    flags, fields, mask, left, right, got_fwd, got_bwd, metric, w_first, w_mid, w_last, biases, out,
    ext, h_a, h_b, stress, w_big, w_hid, w_out, bias_cols,
):
    chans = fields.shape[0] + 1
    feeds = chans - 1
    span_x, span_y = mask.shape
    wide = span_x + 2 * HALO
    taps, hid, _ = w_first.shape
    n_mid = w_mid.shape[0]
    lanes = 2 * span_y

    first = flags[0] == 1
    lo = jnp.where(first, got_fwd[...], got_bwd[...]).astype(F32)
    hi = jnp.where(first, got_bwd[...], got_fwd[...]).astype(F32)
    lane = iota((wide, span_y), 1)
    ext[:, :HALO, :] = jnp.zeros((chans, HALO, lanes), F32)
    ext[:, HALO + wide :, :] = jnp.zeros((chans, HALO, lanes), F32)
    for c in range(chans):
        own = fields[c].astype(F32) if c < chans - 1 else mask[...].astype(F32)
        ext[c, HALO : 2 * HALO, :span_y] = left[c].astype(F32)
        ext[c, BASE : BASE + span_x, :span_y] = own
        ext[c, BASE + span_x : BASE + span_x + HALO, :span_y] = right[c].astype(F32)
        above = pltpu.roll(hi, span_y - c * HALO, 1) if c else hi
        below = pltpu.roll(lo, span_y - (c + 1) * HALO, 1)
        ext[c, HALO : HALO + wide, span_y:] = jnp.where(lane < HALO, above, below)

    depth = taps * feeds * 8
    spread = jnp.zeros((hid, depth), F32)
    for t in range(taps):
        a, b = iota((feeds, depth), 0), iota((feeds, depth), 1)
        place = (b // 8 == t * feeds + a).astype(BF16)
        spread = spread + jnp.dot(w_first[t], place, preferred_element_type=F32)
    sub = iota((hid, depth), 1) % 8
    for r in range(8):
        w_big[r * hid : (r + 1) * hid, :] = jnp.where(sub == r, spread, 0.0).astype(BF16)
    w_out[...] = jnp.zeros_like(w_out)
    for t in range(taps):
        w_out[: w_last.shape[1], t * hid : (t + 1) * hid] = w_last[t]
        for k in range(n_mid):
            w_hid[k, :, t * hid : (t + 1) * hid] = w_mid[k, t]
    for k in range(n_mid + 1):
        a, b = iota((hid, hid), 0), iota((hid, hid), 1)
        row = jnp.broadcast_to(biases[k : k + 1, :], (hid, hid))
        col = jnp.sum(jnp.where(a == b, row, 0.0), axis=1, keepdims=True)
        bias_cols[k] = jnp.broadcast_to(col, (hid, lanes))

    def turn(v, by):
        return pltpu.roll(v, by % lanes, v.ndim - 1)

    def finish(summed, k, row, dst):
        v = (jax.nn.relu(summed + bias_cols[k]) * ext[chans - 1, pl.ds(row, 1), :]).astype(BF16)
        dst[0, row] = v
        dst[1, row] = turn(v, 1)
        dst[2, row] = turn(v, -1)

    def first_step(i, _):
        row = HALO + 8 * i
        pieces = [[] for _ in range(taps)]
        for c in range(feeds):
            window = ext[c, pl.ds(pl.multiple_of(row - 8, 8), 24), :]
            west, here, east = window[7:15], window[8:16], window[9:17]
            pieces[0].append(turn(west, 1) + turn(east, -1))
            pieces[1].append(west + east)
            pieces[2].append(turn(west, -1) + turn(east, 1))
            pieces[3].append(turn(here, 1) + turn(here, -1))
            pieces[4].append(here)
        tapped = jnp.concatenate([p for t in pieces for p in t], axis=0).astype(BF16)
        summed = jnp.dot(w_big[...], tapped, preferred_element_type=F32)
        for r in range(8):
            finish(summed[r * hid : (r + 1) * hid], 0, row + r, h_a)
        return 0

    lax.fori_loop(0, wide // 8, first_step, 0, unroll=2)

    def tapped_row(src, row):
        return jnp.concatenate(
            [
                src[1, row - 1] + src[2, row + 1],
                src[0, row - 1] + src[0, row + 1],
                src[2, row - 1] + src[1, row + 1],
                src[1, row] + src[2, row],
                src[0, row],
            ],
            axis=0,
        )

    src, dst = h_a, h_b
    for k in range(n_mid):
        reach = n_mid + 1 - k

        def step(i, _, k=k, src=src, dst=dst, reach=reach):
            for u in range(UNROLL):
                row = BASE - reach + UNROLL * i + u
                summed = jnp.dot(w_hid[k], tapped_row(src, row), preferred_element_type=F32)
                finish(summed, k + 1, row, dst)
            return 0

        lax.fori_loop(0, -(-(span_x + 2 * reach) // UNROLL), step, 0)
        src, dst = dst, src

    def last_step(i, _):
        for u in range(UNROLL):
            row = BASE - 1 + UNROLL * i + u
            summed = jnp.dot(w_out[...], tapped_row(src, row), preferred_element_type=F32)
            v = (summed[:8] * ext[chans - 1, pl.ds(row, 1), :]).astype(BF16).astype(F32)
            for c in range(3):
                stress[c, pl.ds(row, 1), :] = v[c : c + 1]
        return 0

    lax.fori_loop(0, -(-(span_x + 2) // UNROLL), last_step, 0)

    half_x = metric[0:1, :] * 0.5
    half_y = metric[1:2, :] * 0.5
    ocean = mask[...].astype(F32)

    def diff_x(c):
        east = stress[c, BASE + 1 : BASE + 1 + span_x, :span_y]
        west = stress[c, BASE - 1 : BASE - 1 + span_x, :span_y]
        return (east - west) * half_x

    def diff_y(c):
        here = stress[c, BASE : BASE + span_x, :]
        return (turn(here, -1) - turn(here, 1))[:, :span_y] * half_y

    out[0] = (diff_x(0) + diff_y(1)) * ocean
    out[1] = (diff_x(1) + diff_y(2)) * ocean


def specs(n, vmem=pltpu.VMEM):
    return [pl.BlockSpec(memory_space=pltpu.SMEM)] + [pl.BlockSpec(memory_space=vmem)] * n


def pack(flags, fields, mask, left, right):
    wide, span_y = mask.shape[0] + 2 * HALO, mask.shape[1]
    return pl.pallas_call(
        pack_kernel,
        out_shape=[jax.ShapeDtypeStruct((wide, span_y), BF16)] * 2,
        in_specs=specs(4),
        out_specs=[pl.BlockSpec(memory_space=pltpu.VMEM)] * 2,
        name="pack_rows",
    )(flags, fields, mask, left, right)


def convolve(flags, fields, mask, left, right, got_fwd, got_bwd, metric, w_first, w_mid, w_last, biases):
    span_x, span_y = mask.shape
    rows = span_x + 4 * HALO
    lanes = 2 * span_y
    taps, hid, feeds = w_first.shape
    n_mid = w_mid.shape[0]
    return pl.pallas_call(
        main_kernel,
        out_shape=jax.ShapeDtypeStruct((2, span_x, span_y), F32),
        in_specs=specs(11),
        out_specs=pl.BlockSpec(memory_space=pltpu.VMEM),
        scratch_shapes=[
            pltpu.VMEM((feeds + 1, rows, lanes), F32),
            pltpu.VMEM((3, rows, hid, lanes), BF16),
            pltpu.VMEM((3, rows, hid, lanes), BF16),
            pltpu.VMEM((3, rows, lanes), F32),
            pltpu.VMEM((8 * hid, taps * feeds * 8), BF16),
            pltpu.VMEM((n_mid, hid, taps * hid), BF16),
            pltpu.VMEM((16, taps * hid), BF16),
            pltpu.VMEM((n_mid + 1, hid, lanes), F32),
        ],
        compiler_params=pltpu.CompilerParams(vmem_limit_bytes=40 * 1024 * 1024),
        name="convolve",
    )(flags, fields, mask, left, right, got_fwd, got_bwd, metric, w_first, w_mid, w_last, biases)


def chain(count_x, count_y):
    at = lambda g, y: g * count_y + y
    pairs = []
    for g in range(count_x // 2):
        m = count_x - 1 - g
        pairs += [(at(g, y), at(g, y + 1)) for y in range(count_y - 1)]
        pairs += [(at(g, count_y - 1), at(m, count_y - 1))]
        pairs += [(at(m, y + 1), at(m, y)) for y in range(count_y - 1)]
    return pairs


def on_device(fields, ocean_mask, metric, w_first, w_mid, w_last, biases):
    count_x, count_y = lax.axis_size("gx"), lax.axis_size("gy")
    first = lax.axis_index("gx") < count_x // 2
    fold = lax.axis_index("gy") == count_y - 1
    flags = jnp.stack([first, fold]).astype(jnp.int32)
    span_x = fields.shape[1]

    def edge(start):
        mask_part = ocean_mask[start : start + HALO].astype(BF16)[None]
        return jnp.concatenate([fields[:, start : start + HALO], mask_part], axis=0)

    east = [(i, (i + 1) % count_x) for i in range(count_x)]
    west = [(target, source) for source, target in east]
    left = lax.ppermute(edge(span_x - HALO), "gx", east)
    right = lax.ppermute(edge(0), "gx", west)
    fwd, bwd = pack(flags, fields, ocean_mask, left, right)
    pairs = chain(count_x, count_y)
    got_fwd = lax.ppermute(fwd, ("gx", "gy"), pairs)
    got_bwd = lax.ppermute(bwd, ("gx", "gy"), [(target, source) for source, target in pairs])
    return convolve(
        flags, fields, ocean_mask, left, right, got_fwd, got_bwd, metric, w_first, w_mid, w_last, biases
    )


def solution(mesh):
    placed = (P(None, "gx", "gy"), P("gx", "gy"), P(None, "gy"), P(), P(), P(), P())
    return jax.shard_map(
        on_device, mesh=mesh, in_specs=placed, out_specs=P(None, "gx", "gy"), check_vma=False
    )
```

```python
import jax
import jax.numpy as jnp
from jax import lax
from jax.experimental import pallas as pl
from jax.experimental.pallas import tpu as pltpu
from jax.sharding import PartitionSpec as P

HALO = 8
BASE = 2 * HALO
ONES = 16
STRIP = 32
F32 = jnp.float32
BF16 = jnp.bfloat16
ALONG_X = (0, 1, 2, 3, 4)
ALONG_Y = (0, 3, 2, 1, 4)
VMEM = pl.BlockSpec(memory_space=pltpu.VMEM)


def iota(shape, dim):
    return lax.broadcasted_iota(jnp.int32, shape, dim)


def sides(fields, mask, got_in, got_out):
    chans = fields.shape[0] + 1
    odd = lax.rem(lax.axis_index("gx"), 2)
    west, own, east = [], [], []
    for c in range(chans):
        near = got_in[1 - odd, c]
        far = got_out[odd, c]
        near_low, near_high = near[:HALO].astype(F32), near[HALO:].astype(F32)
        far_low, far_high = far[:HALO].astype(F32), far[HALO:].astype(F32)
        west.append(jnp.where(odd == 1, near_high, far_high))
        east.append(jnp.where(odd == 1, far_low, near_low))
        own.append(fields[c].astype(F32) if c < chans - 1 else mask[...].astype(F32))
    return west, own, east


def pack_kernel(fields, mask, got_in, got_out, pay_in, pay_out, own_low, own_top):
    chans = fields.shape[0] + 1
    span_x, span_y = mask.shape
    wide = span_x + 2 * HALO
    lat, last = lax.axis_index("gy"), lax.axis_size("gy") - 1
    odd = lax.rem(lat, 2) == 1
    west, own, east = sides(fields, mask, got_in, got_out)
    pad = jnp.zeros((span_y - wide, span_y), F32)
    slot = 4 * HALO
    lane = iota((wide, span_y), 1)
    low, top = [], []
    for first in range(0, chans, span_y // slot):
        group = range(first, min(first + span_y // slot, chans))
        gathered = jnp.zeros((wide, span_y), F32)
        for i, c in enumerate(group):
            col = jnp.concatenate([west[c], own[c], east[c]], axis=0)
            here = (lane >= i * slot) & (lane < (i + 1) * slot)
            gathered = jnp.where(here, turn(col, i * slot + 2 * HALO), gathered)
        turned = jnp.concatenate([gathered, pad], axis=0).T
        for i, c in enumerate(group):
            own_top[c] = turned[i * slot : i * slot + 2 * HALO]
            own_low[c] = turned[i * slot + 2 * HALO : (i + 1) * slot]
            top.append(turned[i * slot + HALO : i * slot + 2 * HALO])
            low.append(turned[i * slot + 2 * HALO : i * slot + 3 * HALO])
    low = jnp.concatenate(low, axis=0)
    top = jnp.concatenate(top, axis=0)
    a, b = iota((span_y, span_y), 0), iota((span_y, span_y), 1)
    flip_x = (a + b == wide - 1).astype(BF16)
    a, b = iota((chans * HALO, chans * HALO), 0), iota((chans * HALO, chans * HALO), 1)
    flip_y = ((a // HALO == b // HALO) & (a % HALO + b % HALO == HALO - 1)).astype(BF16)
    mirrored = jnp.dot(top.astype(BF16), flip_x, preferred_element_type=F32).astype(BF16)
    mirrored = jnp.dot(flip_y, mirrored, preferred_element_type=F32)
    out_top = jnp.where(lat == last, mirrored, top)
    for c in range(chans):
        part = slice(c * HALO, (c + 1) * HALO)
        pay_in[c] = jnp.where(odd, low[part], top[part]).astype(BF16)
        pay_out[c] = jnp.where(odd, out_top[part], low[part]).astype(BF16)


def ones_rows(lanes):
    return (iota((ONES, lanes), 0) < 3).astype(BF16)


def turn(v, by):
    return pltpu.roll(v, by % v.shape[-1], v.ndim - 1)


def first_taps(window, order):
    pieces = [[] for _ in range(5)]
    for w in window:
        west, here, east = w[7:15], w[8:16], w[9:17]
        pieces[0].append(turn(west, 1) + turn(east, -1))
        pieces[1].append(west + east)
        pieces[2].append(turn(west, -1) + turn(east, 1))
        pieces[3].append(turn(here, 1) + turn(here, -1))
        pieces[4].append(here)
    stacked = jnp.concatenate([p for t in order for p in pieces[t]], axis=0).astype(BF16)
    return jnp.concatenate([stacked, ones_rows(stacked.shape[1])], axis=0)


def hidden_taps(load, row, order):
    parts = [
        load(1, row - 1) + load(2, row + 1),
        load(0, row - 1) + load(0, row + 1),
        load(2, row - 1) + load(1, row + 1),
        load(1, row) + load(2, row),
        load(0, row),
    ]
    return jnp.concatenate([parts[t] for t in order] + [ones_rows(parts[0].shape[1])], axis=0)


def loader(src):
    seen = {}

    def load(version, row):
        if (version, row) not in seen:
            seen[version, row] = src[version, row]
        return seen[version, row]

    return load


def activate(summed, ocean_row):
    ocean = jnp.broadcast_to(ocean_row, (16, ocean_row.shape[1])).astype(BF16)
    ocean = jnp.concatenate([ocean] * (summed.shape[0] // 16), axis=0)
    return jnp.maximum(summed.astype(BF16), jnp.zeros((), BF16)) * ocean


def put(dst, row, v):
    dst[0, row] = v
    dst[1, row] = turn(v, 1)
    dst[2, row] = turn(v, -1)


def bias_columns(biases, k):
    hid = biases.shape[1]
    a, b = iota((hid, hid), 0), iota((hid, hid), 1)
    row = jnp.broadcast_to(biases[k : k + 1, :], (hid, hid))
    rest = jnp.sum(jnp.where(a == b, row, 0.0), axis=1, keepdims=True)
    spread = jnp.zeros((hid, ONES), F32)
    at = iota((hid, ONES), 1)
    for i in range(3):
        piece = rest.astype(BF16).astype(F32)
        spread = jnp.where(at == i, jnp.broadcast_to(piece, (hid, ONES)), spread)
        rest = rest - piece
    return spread


def arrange_weights(w_first, w_mid, w_last, biases, big, hidden, final):
    taps, hid, feeds = w_first.shape
    n_mid = w_mid.shape[0]
    depth = taps * feeds * 8
    final[...] = jnp.zeros_like(final)
    spread = jnp.zeros((hid, depth), F32)
    for t in range(taps):
        a, b = iota((feeds, depth), 0), iota((feeds, depth), 1)
        place = (b // 8 == t * feeds + a).astype(BF16)
        spread = spread + jnp.dot(w_first[t], place, preferred_element_type=F32)
        final[: w_last.shape[1], t * hid : (t + 1) * hid] = w_last[t]
        for k in range(n_mid):
            hidden[k, :, t * hid : (t + 1) * hid] = w_mid[k, t]
    sub = iota((hid, depth), 1) % 8
    first_bias = bias_columns(biases, 0).astype(BF16)
    for r in range(8):
        big[r * hid : (r + 1) * hid, :depth] = jnp.where(sub == r, spread, 0.0).astype(BF16)
        big[r * hid : (r + 1) * hid, depth:] = first_bias
    for k in range(n_mid):
        hidden[k, :, taps * hid :] = bias_columns(biases, k + 1).astype(BF16)


def main_kernel(
    fields, mask, got_in, got_out, w_first, w_mid, w_last, biases, stress, big, hidden, final, ext, h_a, h_b
):
    chans = fields.shape[0] + 1
    feeds = chans - 1
    span_x, span_y = mask.shape
    n_mid, hid, _ = hidden.shape
    arrange_weights(w_first, w_mid, w_last, biases, big, hidden, final)
    west, own, east = sides(fields, mask, got_in, got_out)
    nothing = jnp.zeros((HALO, span_y), F32)
    for c in range(chans):
        ext[c, :HALO] = nothing
        ext[c, HALO:BASE] = west[c]
        ext[c, BASE : BASE + span_x] = own[c]
        ext[c, BASE + span_x : BASE + span_x + HALO] = east[c]
        ext[c, BASE + span_x + HALO :] = nothing

    def ocean_row(row):
        return ext[chans - 1, row : row + 1, :]

    def halves(v):
        return v[:, :span_y], v[:, span_y:]

    for start in range(HALO, BASE + span_x + HALO, 16):
        taps = [
            first_taps([ext[c, row - 8 : row + 16, :] for c in range(feeds)], ALONG_X)
            for row in (start, start + 8)
        ]
        summed = jnp.dot(big[...], jnp.concatenate(taps, axis=1), preferred_element_type=F32)
        for part, row in zip(halves(summed), (start, start + 8)):
            for r in range(8):
                put(h_a, row + r, activate(part[r * hid : (r + 1) * hid], ocean_row(row + r)))

    def layer(weights, src, reach, finish):
        cached = loader(src)
        for start in range(BASE - reach, BASE + span_x + reach, 2):
            taps = [hidden_taps(cached, row, ALONG_X) for row in (start, start + 1)]
            summed = jnp.dot(weights, jnp.concatenate(taps, axis=1), preferred_element_type=F32)
            for part, row in zip(halves(summed), (start, start + 1)):
                finish(part, row)

    src, dst = h_a, h_b
    for k in range(n_mid):
        layer(hidden[k], src, n_mid + 1 - k, lambda v, row: put(dst, row, activate(v, ocean_row(row))))
        src, dst = dst, src

    def finish(summed, row):
        v = (summed[:8] * ocean_row(row)).astype(BF16).astype(F32)
        for c in range(3):
            stress[c, row : row + 1, :] = v[c : c + 1]

    layer(final[...], src, 1, finish)


def strip_kernel(
    own_low, own_top, got_in, got_out, stress, big, hidden, final, mask, metric, out, ext, h_a, h_b, edge
):
    chans = own_low.shape[0]
    feeds = chans - 1
    span_x, span_y = mask.shape
    n_mid, hid, _ = hidden.shape
    odd = lax.rem(lax.axis_index("gy"), 2) == 1
    ext[...] = jnp.zeros_like(ext)
    for c in range(chans):
        inner, outer = got_in[c].astype(F32), got_out[c].astype(F32)
        below = jnp.where(odd, inner, outer)
        above = jnp.where(odd, outer, inner)
        ext[c, 6:14, :span_y] = below
        ext[c, 14:30, :span_y] = own_low[c]
        ext[c, 2:18, span_y:] = own_top[c]
        ext[c, 18:26, span_y:] = above

    def ocean_row(row):
        return ext[chans - 1, row : row + 1, :]

    def put_both(dst, row, v):
        for half in range(2):
            lanes = slice(half * span_y, (half + 1) * span_y)
            part = v[:, lanes]
            dst[0, row, :, lanes] = part
            dst[1, row, :, lanes] = turn(part, 1)
            dst[2, row, :, lanes] = turn(part, -1)

    for row in (8, 16):
        taps = [
            first_taps([ext[c, row - 8 : row + 16, half * span_y : (half + 1) * span_y] for c in range(feeds)], ALONG_Y)
            for half in range(2)
        ]
        summed = jnp.dot(big[...], jnp.concatenate(taps, axis=1), preferred_element_type=F32)
        for r in range(8):
            put_both(h_a, row + r, activate(summed[r * hid : (r + 1) * hid], ocean_row(row + r)))

    src, dst = h_a, h_b
    for k in range(n_mid):
        cached = loader(src)
        for row in range(10 + k, 22 - k):
            taps = hidden_taps(cached, row, ALONG_Y)
            summed = jnp.dot(hidden[k], taps, preferred_element_type=F32)
            put_both(dst, row, activate(summed, ocean_row(row)))
        src, dst = dst, src
    edge[...] = jnp.zeros_like(edge)
    cached = loader(src)
    for row in range(13, 19):
        summed = jnp.dot(final[...], hidden_taps(cached, row, ALONG_Y), preferred_element_type=F32)
        v = (summed[:8] * ocean_row(row)).astype(BF16).astype(F32)
        low, high = row - 14, span_y - 18 + row
        for c in range(3):
            for lat, part in ((low, v[c : c + 1, :span_y]), (high, v[c : c + 1, span_y:])):
                tile, slot = (0, lat) if 0 <= lat < span_y else (1, lat % span_y)
                edge[c, tile, slot : slot + 1, :] = part

    half_x = metric[0:1, :] * 0.5
    half_y = metric[1:2, :] * 0.5
    ocean = mask[...].astype(F32)
    lane = iota((span_x + 2, span_y), 1)
    planes, north, south = [], [], []
    for c in range(3):
        inside = edge[c, 0].T[HALO - 1 : HALO + span_x + 1]
        beyond = edge[c, 1].T[HALO : HALO + span_x]
        near = (lane < 5) | (lane >= span_y - 5)
        plane = jnp.where(near, inside, stress[c, BASE - 1 : BASE + span_x + 1, :])
        here = plane[1 : 1 + span_x]
        inner = lane[:span_x]
        planes.append(plane)
        north.append(turn(jnp.where(inner == 0, beyond, here), -1))
        south.append(turn(jnp.where(inner == span_y - 1, beyond, here), 1))

    def diff_x(c):
        return (planes[c][2:] - planes[c][:span_x]) * half_x

    def diff_y(c):
        return (north[c] - south[c]) * half_y

    out[0] = (diff_x(0) + diff_y(1)) * ocean
    out[1] = (diff_x(1) + diff_y(2)) * ocean


def pack(fields, mask, got_in, got_out):
    chans, span_y = fields.shape[0] + 1, mask.shape[1]
    return pl.pallas_call(
        pack_kernel,
        out_shape=[jax.ShapeDtypeStruct((chans, HALO, span_y), BF16)] * 2
        + [jax.ShapeDtypeStruct((chans, 2 * HALO, span_y), F32)] * 2,
        in_specs=[VMEM] * 4,
        out_specs=[VMEM] * 4,
        compiler_params=pltpu.CompilerParams(vmem_limit_bytes=4 * 1024 * 1024),
        name="pack_rows",
    )(fields, mask, got_in, got_out)


def main(fields, mask, got_in, got_out, w_first, w_mid, w_last, biases):
    span_x, span_y = mask.shape
    rows = span_x + 4 * HALO
    taps, hid, feeds = w_first.shape
    n_mid = w_mid.shape[0]
    return pl.pallas_call(
        main_kernel,
        out_shape=[
            jax.ShapeDtypeStruct((3, rows, span_y), F32),
            jax.ShapeDtypeStruct((8 * hid, taps * feeds * 8 + ONES), BF16),
            jax.ShapeDtypeStruct((n_mid, hid, taps * hid + ONES), BF16),
            jax.ShapeDtypeStruct((16, taps * hid + ONES), BF16),
        ],
        in_specs=[VMEM] * 8,
        out_specs=[VMEM] * 4,
        scratch_shapes=[
            pltpu.VMEM((feeds + 1, rows, span_y), F32),
            pltpu.VMEM((3, rows, hid, span_y), BF16),
            pltpu.VMEM((3, rows, hid, span_y), BF16),
        ],
        compiler_params=pltpu.CompilerParams(vmem_limit_bytes=16 * 1024 * 1024),
        cost_estimate=pl.CostEstimate(flops=5_000_000_000, bytes_accessed=20_000_000, transcendentals=0),
        name="own_rows",
    )(fields, mask, got_in, got_out, w_first, w_mid, w_last, biases)


def strips(own_low, own_top, got_in, got_out, stress, big, hidden, final, mask, metric):
    span_x, span_y = mask.shape
    hid = hidden.shape[1]
    return pl.pallas_call(
        strip_kernel,
        out_shape=jax.ShapeDtypeStruct((2, span_x, span_y), F32),
        in_specs=[VMEM] * 10,
        out_specs=VMEM,
        scratch_shapes=[
            pltpu.VMEM((own_low.shape[0], STRIP, 2 * span_y), F32),
            pltpu.VMEM((3, STRIP, hid, 2 * span_y), BF16),
            pltpu.VMEM((3, STRIP, hid, 2 * span_y), BF16),
            pltpu.VMEM((3, 2, span_y, span_y), F32),
        ],
        compiler_params=pltpu.CompilerParams(vmem_limit_bytes=8 * 1024 * 1024),
        name="edge_rows",
    )(own_low, own_top, got_in, got_out, stress, big, hidden, final, mask, metric)


def latitude_pairs(count_x, count_y, across):
    at = lambda g, y: g * count_y + y
    pairs = []
    for g in range(count_x):
        for y in range(count_y):
            up = (y % 2 == 0) != across
            if up and y == count_y - 1:
                pairs.append((at(g, y), at(count_x - 1 - g, y)))
            elif up or y > 0:
                pairs.append((at(g, y), at(g, y + 1 if up else y - 1)))
    return pairs


def on_device(fields, ocean_mask, metric, w_first, w_mid, w_last, biases):
    count_x, count_y = lax.axis_size("gx"), lax.axis_size("gy")
    span_x = fields.shape[1]
    inside = [[i, i + 1] for i in range(0, count_x, 2)]
    across = [[i, (i + 1) % count_x] for i in range(1, count_x, 2)]
    both = jnp.concatenate([fields, ocean_mask.astype(BF16)[None]], axis=0)
    edges = jnp.concatenate([both[:, :HALO], both[:, span_x - HALO :]], axis=1)
    got_in = lax.all_gather(edges, "gx", axis_index_groups=inside)
    got_out = lax.all_gather(edges, "gx", axis_index_groups=across)
    pay_in, pay_out, own_low, own_top = pack(fields, ocean_mask, got_in, got_out)
    lat_in = lax.ppermute(pay_in, ("gx", "gy"), latitude_pairs(count_x, count_y, False))
    lat_out = lax.ppermute(pay_out, ("gx", "gy"), latitude_pairs(count_x, count_y, True))
    stress, big, hidden, final = main(fields, ocean_mask, got_in, got_out, w_first, w_mid, w_last, biases)
    return strips(own_low, own_top, lat_in, lat_out, stress, big, hidden, final, ocean_mask, metric)


def solution(mesh):
    placed = (P(None, "gx", "gy"), P("gx", "gy"), P(None, "gy"), P(), P(), P(), P())
    return jax.shard_map(
        on_device, mesh=mesh, in_specs=placed, out_specs=P(None, "gx", "gy"), check_vma=False
    )
```

```python
import jax
import jax.numpy as jnp
from jax import lax
from jax.experimental import pallas as pl
from jax.experimental.pallas import tpu as pltpu
from jax.sharding import PartitionSpec as P

HALO = 8
EARLY = 8
ONES = 16
STRIP = 32
F32 = jnp.float32
BF16 = jnp.bfloat16
ALONG_X = (0, 1, 2, 3, 4)
ALONG_Y = (0, 3, 2, 1, 4)
VMEM = pl.BlockSpec(memory_space=pltpu.VMEM)


def iota(shape, dim):
    return lax.broadcasted_iota(jnp.int32, shape, dim)


def sides(fields, mask, got_in, got_out):
    chans = fields.shape[0] + 1
    odd = lax.rem(lax.axis_index("gx"), 2)
    west, own, east = [], [], []
    for c in range(chans):
        near = got_in[1 - odd, c]
        far = got_out[odd, c]
        near_low, near_high = near[:HALO].astype(F32), near[HALO:].astype(F32)
        far_low, far_high = far[:HALO].astype(F32), far[HALO:].astype(F32)
        west.append(jnp.where(odd == 1, near_high, far_high))
        east.append(jnp.where(odd == 1, far_low, near_low))
        own.append(fields[c].astype(F32) if c < chans - 1 else mask[...].astype(F32))
    return west, own, east


def edge_kernel(fields, mask, metric, edges, halved):
    feeds, span_x, _ = fields.shape
    for part, start in enumerate((0, span_x - HALO)):
        rows = slice(part * HALO, (part + 1) * HALO)
        edges[:feeds, rows] = fields[:, start : start + HALO]
        edges[feeds, rows] = mask[start : start + HALO]
    halved[...] = metric[...] * 0.5


def pack_kernel(fields, mask, got_in, got_out, pay_in, pay_out, own_low, own_top):
    chans = fields.shape[0] + 1
    span_x, span_y = mask.shape
    wide = span_x + 2 * HALO
    lat, last = lax.axis_index("gy"), lax.axis_size("gy") - 1
    odd = lax.rem(lat, 2) == 1
    west, own, east = sides(fields, mask, got_in, got_out)
    pad = jnp.zeros((span_y - wide, span_y), F32)
    slot = 4 * HALO
    lane = iota((wide, span_y), 1)
    low, top = [], []
    for first in range(0, chans, span_y // slot):
        group = range(first, min(first + span_y // slot, chans))
        gathered = jnp.zeros((wide, span_y), F32)
        for i, c in enumerate(group):
            col = jnp.concatenate([west[c], own[c], east[c]], axis=0)
            here = (lane >= i * slot) & (lane < (i + 1) * slot)
            gathered = jnp.where(here, turn(col, i * slot + 2 * HALO), gathered)
        turned = jnp.concatenate([gathered, pad], axis=0).T
        for i, c in enumerate(group):
            own_top[c] = turned[i * slot : i * slot + 2 * HALO]
            own_low[c] = turned[i * slot + 2 * HALO : (i + 1) * slot]
            top.append(turned[i * slot + HALO : i * slot + 2 * HALO])
            low.append(turned[i * slot + 2 * HALO : i * slot + 3 * HALO])
    low = jnp.concatenate(low, axis=0)
    top = jnp.concatenate(top, axis=0)
    a, b = iota((span_y, span_y), 0), iota((span_y, span_y), 1)
    flip_x = (a + b == wide - 1).astype(BF16)
    a, b = iota((chans * HALO, chans * HALO), 0), iota((chans * HALO, chans * HALO), 1)
    flip_y = ((a // HALO == b // HALO) & (a % HALO + b % HALO == HALO - 1)).astype(BF16)
    mirrored = jnp.dot(top.astype(BF16), flip_x, preferred_element_type=F32).astype(BF16)
    mirrored = jnp.dot(flip_y, mirrored, preferred_element_type=F32)
    out_top = jnp.where(lat == last, mirrored, top)
    for c in range(chans):
        part = slice(c * HALO, (c + 1) * HALO)
        pay_in[c] = jnp.where(odd, low[part], top[part]).astype(BF16)
        pay_out[c] = jnp.where(odd, out_top[part], low[part]).astype(BF16)


def ones_rows(lanes):
    return (iota((ONES, lanes), 0) < 3).astype(BF16)


def turn(v, by):
    return pltpu.roll(v, by % v.shape[-1], v.ndim - 1)


def first_taps(window, order):
    pieces = [[] for _ in range(5)]
    for w in window:
        west, here, east = w[:8], w[1:9], w[2:]
        pieces[0].append(turn(west, 1) + turn(east, -1))
        pieces[1].append(west + east)
        pieces[2].append(turn(west, -1) + turn(east, 1))
        pieces[3].append(turn(here, 1) + turn(here, -1))
        pieces[4].append(here)
    stacked = jnp.concatenate([p for t in order for p in pieces[t]], axis=0).astype(BF16)
    return jnp.concatenate([stacked, ones_rows(stacked.shape[1])], axis=0)


def hidden_taps(load, row, order):
    parts = [
        load(1, row - 1) + load(2, row + 1),
        load(0, row - 1) + load(0, row + 1),
        load(2, row - 1) + load(1, row + 1),
        load(1, row) + load(2, row),
        load(0, row),
    ]
    return jnp.concatenate([parts[t] for t in order] + [ones_rows(parts[0].shape[1])], axis=0)


def loader(src):
    seen = {}

    def load(version, row):
        if (version, row) not in seen:
            seen[version, row] = src[version, row]
        return seen[version, row]

    return load


def activate(summed, ocean_row):
    ocean = jnp.broadcast_to(ocean_row, (16, ocean_row.shape[1])).astype(BF16)
    ocean = jnp.concatenate([ocean] * (summed.shape[0] // 16), axis=0)
    return jnp.maximum(summed.astype(BF16), jnp.zeros((), BF16)) * ocean


def put(dst, row, v):
    dst[0, row] = v
    dst[1, row] = turn(v, 1)
    dst[2, row] = turn(v, -1)


def bias_columns(biases, k):
    hid = biases.shape[1]
    a, b = iota((hid, hid), 0), iota((hid, hid), 1)
    row = jnp.broadcast_to(biases[k : k + 1, :], (hid, hid))
    rest = jnp.sum(jnp.where(a == b, row, 0.0), axis=1, keepdims=True)
    spread = jnp.zeros((hid, ONES), F32)
    at = iota((hid, ONES), 1)
    for i in range(3):
        piece = rest.astype(BF16).astype(F32)
        spread = jnp.where(at == i, jnp.broadcast_to(piece, (hid, ONES)), spread)
        rest = rest - piece
    return spread


def arrange_weights(w_first, w_mid, w_last, biases, big, hidden, final):
    taps, feeds, hid = w_first.shape
    n_mid = w_mid.shape[0]
    depth = taps * feeds * 8
    final[...] = jnp.zeros_like(final)
    lanes = 128
    stacked = [w_first[t].astype(F32) for t in range(taps)]
    stacked = jnp.concatenate(stacked + [jnp.zeros((lanes - taps * feeds, hid), F32)], axis=0)
    stacked = jnp.concatenate([stacked, jnp.zeros((lanes, lanes - hid), F32)], axis=1).T
    a, b = iota((lanes, depth), 0), iota((lanes, depth), 1)
    place = (b // 8 == a).astype(BF16)
    spread = jnp.dot(stacked[:hid].astype(BF16), place, preferred_element_type=F32)
    for t in range(taps):
        final[: w_last.shape[1], t * hid : (t + 1) * hid] = w_last[t]
        for k in range(n_mid):
            hidden[k, :, t * hid : (t + 1) * hid] = w_mid[k, t]
    sub = iota((hid, depth), 1) % 8
    first_bias = bias_columns(biases, 0).astype(BF16)
    for r in range(8):
        big[r * hid : (r + 1) * hid, :depth] = jnp.where(sub == r, spread, 0.0).astype(BF16)
        big[r * hid : (r + 1) * hid, depth:] = first_bias
    for k in range(n_mid):
        hidden[k, :, taps * hid :] = bias_columns(biases, k + 1).astype(BF16)


def waits_long():
    place = lax.rem(lax.axis_index("gx"), lax.axis_size("gx") // 4)
    top = lax.axis_index("gy") == lax.axis_size("gy") - 1
    origin = (lax.axis_index("gx") == 0) & (lax.axis_index("gy") == 0)
    return jnp.logical_not(origin) & ((place == 0) | (top & (place < EARLY)))


def halves(v):
    half = v.shape[1] // 2
    return v[:, :half], v[:, half:]


def masked_stress(summed, ocean_row):
    return (summed[:8] * ocean_row).astype(BF16).astype(F32)


def inner_columns(fields, mask, w_first, w_mid, w_last, biases, stress, kept, big, hidden, final, ext, h_a, h_b):
    feeds, span_x, span_y = fields.shape
    n_mid = w_mid.shape[0]
    hid = w_first.shape[2]
    arrange_weights(w_first, w_mid, w_last, biases, big, hidden, final)
    for c in range(feeds):
        ext[c, :HALO] = jnp.zeros((HALO, span_y), F32)
        ext[c, HALO : HALO + span_x] = fields[c].astype(F32)
        ext[c, HALO + span_x :] = jnp.zeros((HALO, span_y), F32)
    ext[feeds, HALO : HALO + span_x] = mask[...].astype(F32)

    def ocean_row(row):
        return ext[feeds, HALO + row : HALO + row + 1, :]

    def keep(k, row, v):
        for slot, at in enumerate((k, k + 1, span_x - k - 2, span_x - k - 1)):
            if row == at:
                kept[k - 1, slot] = v

    for start in range(0, span_x, 16):
        taps = [
            first_taps([ext[c, HALO + row - 1 : HALO + row + 9, :] for c in range(feeds)], ALONG_X)
            for row in (start, start + 8)
        ]
        summed = jnp.dot(big[...], jnp.concatenate(taps, axis=1), preferred_element_type=F32)
        for part, row in zip(halves(summed), (start, start + 8)):
            for r in range(8):
                v = activate(part[r * hid : (r + 1) * hid], ocean_row(row + r))
                put(h_a, row + r, v)
                keep(1, row + r, v)

    def layer(weights, src, k, finish):
        cached = loader(src)
        for start in range(k, span_x - k, 2):
            taps = [hidden_taps(cached, row, ALONG_X) for row in (start, start + 1)]
            summed = jnp.dot(weights, jnp.concatenate(taps, axis=1), preferred_element_type=F32)
            for part, row in zip(halves(summed), (start, start + 1)):
                finish(part, row)

    src, dst = h_a, h_b
    for k in range(2, n_mid + 2):

        def finish(summed, row):
            v = activate(summed, ocean_row(row))
            put(dst, row, v)
            keep(k, row, v)

        layer(hidden[k - 2], src, k, finish)
        src, dst = dst, src

    def finish(summed, row):
        v = masked_stress(summed, ocean_row(row))
        for c in range(3):
            stress[c, HALO + row : HALO + row + 1, :] = v[c : c + 1]

    layer(final[...], src, n_mid + 2, finish)


def early_kernel(
    edges, got_in, fields, mask, w_first, w_mid, w_last, biases,
    edges_out, stress, kept, big, hidden, final, ext, h_a, h_b,
):
    del got_in
    edges_out[...] = edges[...]

    @pl.when(waits_long())
    def _():
        inner_columns(
            fields, mask, w_first, w_mid, w_last, biases, stress, kept, big, hidden, final, ext, h_a, h_b
        )


def side_kernel(
    fields, mask, got_in, got_out, w_first, w_mid, w_last, biases, stress_in, kept_in, big_in, hidden_in, final_in,
    stress, big, hidden, final, ext, h_a, h_b, rows_a, rows_b, kept,
):
    feeds, span_x, span_y = fields.shape
    n_mid = w_mid.shape[0]
    hid = w_first.shape[2]

    @pl.when(waits_long())
    def _():
        for done, here in ((stress_in, stress), (kept_in, kept), (big_in, big), (hidden_in, hidden), (final_in, final)):
            here[...] = done[...]

    @pl.when(jnp.logical_not(waits_long()))
    def _():
        inner_columns(
            fields, mask, w_first, w_mid, w_last, biases, stress, kept, big, hidden, final, ext, h_a, h_b
        )

    west, own, east = sides(fields, mask, got_in, got_out)
    for c in range(feeds + 1):
        ext[c, :HALO] = west[c]
        ext[c, HALO : HALO + span_x] = own[c]
        ext[c, HALO + span_x :] = east[c]

    def places(k, slot):
        return k - 8 + slot, span_x - 2 - k + slot

    def ocean_row(row):
        return ext[feeds, HALO + row : HALO + row + 1, :]

    def fill(dst, k):
        for slot in range(2):
            put(dst.at[0], 8 + slot, kept[k - 1, slot])
            put(dst.at[1], slot, kept[k - 1, 2 + slot])

    starts = (-6, span_x - 2)
    taps = [
        first_taps([ext[c, HALO + row - 1 : HALO + row + 9, :] for c in range(feeds)], ALONG_X)
        for row in starts
    ]
    summed = jnp.dot(big[...], jnp.concatenate(taps, axis=1), preferred_element_type=F32)
    for side, part in enumerate(halves(summed)):
        for slot in range(2, 8):
            row = places(1, slot)[side]
            r = row - starts[side]
            put(rows_a.at[side], slot, activate(part[r * hid : (r + 1) * hid], ocean_row(row)))
    fill(rows_a, 1)

    src, dst = rows_a, rows_b
    for k in range(2, n_mid + 3):
        loads = [loader(src.at[side]) for side in range(2)]
        weights = hidden[k - 2] if k < n_mid + 2 else final[...]
        for slot in range(2, 8):
            taps = [hidden_taps(loads[0], slot + 1, ALONG_X), hidden_taps(loads[1], slot - 1, ALONG_X)]
            summed = jnp.dot(weights, jnp.concatenate(taps, axis=1), preferred_element_type=F32)
            for side, part in enumerate(halves(summed)):
                row = places(k, slot)[side]
                if k < n_mid + 2:
                    put(dst.at[side], slot, activate(part, ocean_row(row)))
                else:
                    v = masked_stress(part, ocean_row(row))
                    for c in range(3):
                        stress[c, HALO + row : HALO + row + 1, :] = v[c : c + 1]
        if k < n_mid + 2:
            fill(dst, k)
        src, dst = dst, src


def strip_kernel(
    own_low, own_top, got_in, got_out, stress, big, hidden, final, mask, halved, out, ext, h_a, h_b, edge
):
    chans = own_low.shape[0]
    feeds = chans - 1
    span_x, span_y = mask.shape
    n_mid, hid, _ = hidden.shape
    odd = lax.rem(lax.axis_index("gy"), 2) == 1
    ext[...] = jnp.zeros_like(ext)
    for c in range(chans):
        inner, outer = got_in[c].astype(F32), got_out[c].astype(F32)
        below = jnp.where(odd, inner, outer)
        above = jnp.where(odd, outer, inner)
        ext[c, 6:14, :span_y] = below
        ext[c, 14:30, :span_y] = own_low[c]
        ext[c, 2:18, span_y:] = own_top[c]
        ext[c, 18:26, span_y:] = above

    def ocean_row(row):
        return ext[chans - 1, row : row + 1, :]

    def put_both(dst, row, v):
        for half in range(2):
            lanes = slice(half * span_y, (half + 1) * span_y)
            part = v[:, lanes]
            dst[0, row, :, lanes] = part
            dst[1, row, :, lanes] = turn(part, 1)
            dst[2, row, :, lanes] = turn(part, -1)

    for row in (8, 16):
        taps = [
            first_taps([ext[c, row - 1 : row + 9, half * span_y : (half + 1) * span_y] for c in range(feeds)], ALONG_Y)
            for half in range(2)
        ]
        summed = jnp.dot(big[...], jnp.concatenate(taps, axis=1), preferred_element_type=F32)
        for r in range(8):
            put_both(h_a, row + r, activate(summed[r * hid : (r + 1) * hid], ocean_row(row + r)))

    src, dst = h_a, h_b
    for k in range(n_mid):
        cached = loader(src)
        for row in range(10 + k, 22 - k):
            taps = hidden_taps(cached, row, ALONG_Y)
            summed = jnp.dot(hidden[k], taps, preferred_element_type=F32)
            put_both(dst, row, activate(summed, ocean_row(row)))
        src, dst = dst, src
    slot = 2 * HALO
    cached = loader(src)
    for row in range(13, 19):
        summed = jnp.dot(final[...], hidden_taps(cached, row, ALONG_Y), preferred_element_type=F32)
        v = masked_stress(summed, ocean_row(row))
        for c in range(3):
            edge[c * slot + row - 13 : c * slot + row - 12, :] = v[c : c + 1, :span_y]
            edge[c * slot + row - 5 : c * slot + row - 4, :] = v[c : c + 1, span_y:]
    turned = edge[...].T[HALO - 1 : HALO + span_x + 1]

    half_x = halved[0:1, :]
    half_y = halved[1:2, :]
    ocean = mask[...].astype(F32)
    lane = iota((span_x + 2, span_y), 1)
    inner = lane[:span_x]
    planes, north, south = [], [], []
    for c in range(3):
        low = turn(turned, -(c * slot + 1))
        high = turn(turned, span_y - 5 - (c * slot + HALO))
        plane = jnp.where(lane < 5, low, jnp.where(lane >= span_y - 5, high, stress[c, HALO - 1 : HALO + span_x + 1, :]))
        here = plane[1 : 1 + span_x]
        beyond = turn(turned[1 : 1 + span_x], span_y - 1 - (c * slot + HALO + 5))
        below = turn(turned[1 : 1 + span_x], -c * slot)
        planes.append(plane)
        north.append(jnp.where(inner == span_y - 1, beyond, turn(here, -1)))
        south.append(jnp.where(inner == 0, below, turn(here, 1)))

    def diff_x(c):
        return (planes[c][2:] - planes[c][:span_x]) * half_x

    def diff_y(c):
        return (north[c] - south[c]) * half_y

    out[0] = (diff_x(0) + diff_y(1)) * ocean
    out[1] = (diff_x(1) + diff_y(2)) * ocean


def pack(fields, mask, got_in, got_out):
    chans, span_y = fields.shape[0] + 1, mask.shape[1]
    return pl.pallas_call(
        pack_kernel,
        out_shape=[jax.ShapeDtypeStruct((chans, HALO, span_y), BF16)] * 2
        + [jax.ShapeDtypeStruct((chans, 2 * HALO, span_y), F32)] * 2,
        in_specs=[VMEM] * 4,
        out_specs=[VMEM] * 4,
        compiler_params=pltpu.CompilerParams(vmem_limit_bytes=4 * 1024 * 1024),
        name="pack_rows",
    )(fields, mask, got_in, got_out)


def outermost(fields, mask, metric):
    return pl.pallas_call(
        edge_kernel,
        out_shape=[
            jax.ShapeDtypeStruct((fields.shape[0] + 1, 2 * HALO, fields.shape[2]), BF16),
            jax.ShapeDtypeStruct(metric.shape, F32),
        ],
        in_specs=[VMEM] * 3,
        out_specs=[VMEM] * 2,
        compiler_params=pltpu.CompilerParams(vmem_limit_bytes=4 * 1024 * 1024),
        cost_estimate=pl.CostEstimate(flops=10_000_000_000, bytes_accessed=1_000_000, transcendentals=0),
        name="outermost_columns",
    )(fields, mask, metric)


def inner_shapes(fields, w_first, w_mid):
    feeds, span_x, span_y = fields.shape
    taps, _, hid = w_first.shape
    n_mid = w_mid.shape[0]
    rows = span_x + 2 * HALO
    outs = [
        jax.ShapeDtypeStruct((3, rows, span_y), F32),
        jax.ShapeDtypeStruct((n_mid + 1, 4, hid, span_y), BF16),
        jax.ShapeDtypeStruct((8 * hid, taps * feeds * 8 + ONES), BF16),
        jax.ShapeDtypeStruct((n_mid, hid, taps * hid + ONES), BF16),
        jax.ShapeDtypeStruct((16, taps * hid + ONES), BF16),
    ]
    scratch = [
        pltpu.VMEM((feeds + 1, rows, span_y), F32),
        pltpu.VMEM((3, span_x, hid, span_y), BF16),
        pltpu.VMEM((3, span_x, hid, span_y), BF16),
    ]
    return outs, scratch


def early(edges, got_in, fields, mask, w_first, w_mid, w_last, biases):
    outs, scratch = inner_shapes(fields, w_first, w_mid)
    return pl.pallas_call(
        early_kernel,
        out_shape=[jax.ShapeDtypeStruct(edges.shape, edges.dtype)] + outs,
        in_specs=[VMEM] * 8,
        out_specs=[VMEM] * 6,
        scratch_shapes=scratch,
        compiler_params=pltpu.CompilerParams(vmem_limit_bytes=12 * 1024 * 1024),
        name="inner_early",
    )(edges, got_in, fields, mask, w_first, w_mid, w_last, biases)


def side_columns(fields, mask, got_in, got_out, w_first, w_mid, w_last, biases, done):
    outs, scratch = inner_shapes(fields, w_first, w_mid)
    hid, span_y = w_first.shape[2], mask.shape[1]
    return pl.pallas_call(
        side_kernel,
        out_shape=outs[:1] + outs[2:],
        in_specs=[VMEM] * 13,
        out_specs=[VMEM] * 4,
        scratch_shapes=scratch
        + [pltpu.VMEM((2, 3, 10, hid, span_y), BF16)] * 2
        + [pltpu.VMEM(outs[1].shape, BF16)],
        compiler_params=pltpu.CompilerParams(vmem_limit_bytes=12 * 1024 * 1024),
        cost_estimate=pl.CostEstimate(flops=5_000_000_000, bytes_accessed=20_000_000, transcendentals=0),
        name="inner_and_sides",
    )(fields, mask, got_in, got_out, w_first, w_mid, w_last, biases, *done)


def strips(own_low, own_top, got_in, got_out, stress, big, hidden, final, mask, halved):
    span_x, span_y = mask.shape
    hid = hidden.shape[1]
    return pl.pallas_call(
        strip_kernel,
        out_shape=jax.ShapeDtypeStruct((2, span_x, span_y), F32),
        in_specs=[VMEM] * 10,
        out_specs=VMEM,
        scratch_shapes=[
            pltpu.VMEM((own_low.shape[0], STRIP, 2 * span_y), F32),
            pltpu.VMEM((3, STRIP, hid, 2 * span_y), BF16),
            pltpu.VMEM((3, STRIP, hid, 2 * span_y), BF16),
            pltpu.VMEM((span_y, span_y), F32),
        ],
        compiler_params=pltpu.CompilerParams(vmem_limit_bytes=8 * 1024 * 1024),
        name="edge_rows",
    )(own_low, own_top, got_in, got_out, stress, big, hidden, final, mask, halved)


def latitude_pairs(count_x, count_y, across):
    at = lambda g, y: g * count_y + y
    pairs = []
    for g in range(count_x):
        for y in range(count_y):
            up = (y % 2 == 0) != across
            if up and y == count_y - 1:
                pairs.append((at(g, y), at(count_x - 1 - g, y)))
            elif up or y > 0:
                pairs.append((at(g, y), at(g, y + 1 if up else y - 1)))
    return pairs


def on_device(fields, ocean_mask, metric, w_first, w_mid, w_last, biases):
    count_x, count_y = lax.axis_size("gx"), lax.axis_size("gy")
    inside = [[i, i + 1] for i in range(0, count_x, 2)]
    across = [[i, (i + 1) % count_x] for i in range(1, count_x, 2)]
    weights = (jnp.swapaxes(w_first, 1, 2), w_mid, w_last, biases)
    ocean_mask = ocean_mask.astype(BF16)
    edges, halved = outermost(fields, ocean_mask, metric)
    got_in = lax.all_gather(edges, "gx", axis_index_groups=inside)
    edges, *done = early(edges, got_in, fields, ocean_mask, *weights)
    got_out = lax.all_gather(edges, "gx", axis_index_groups=across)
    pay_in, pay_out, own_low, own_top = pack(fields, ocean_mask, got_in, got_out)
    lat_in = lax.ppermute(pay_in, ("gx", "gy"), latitude_pairs(count_x, count_y, False))
    lat_out = lax.ppermute(pay_out, ("gx", "gy"), latitude_pairs(count_x, count_y, True))
    stress, big, hidden, final = side_columns(fields, ocean_mask, got_in, got_out, *weights, done)
    return strips(own_low, own_top, lat_in, lat_out, stress, big, hidden, final, ocean_mask, halved)


def solution(mesh):
    placed = (P(None, "gx", "gy"), P("gx", "gy"), P(None, "gy"), P(), P(), P(), P())
    return jax.shard_map(
        on_device, mesh=mesh, in_specs=placed, out_specs=P(None, "gx", "gy"), check_vma=False
    )
```

```python
import jax
import jax.numpy as jnp
from jax import lax
from jax.experimental import pallas as pl
from jax.experimental.pallas import tpu as pltpu
from jax.sharding import PartitionSpec as P

HALO = 8
EARLY = 8
ONES = 16
STRIP = 32
F32 = jnp.float32
BF16 = jnp.bfloat16
ALONG_X = (0, 1, 2, 3, 4)
ALONG_Y = (0, 3, 2, 1, 4)
VMEM = pl.BlockSpec(memory_space=pltpu.VMEM)


def iota(shape, dim):
    return lax.broadcasted_iota(jnp.int32, shape, dim)


def sides(fields, mask, got_in, got_out):
    chans = fields.shape[0] + 1
    odd = lax.rem(lax.axis_index("gx"), 2)
    west, own, east = [], [], []
    for c in range(chans):
        near = got_in[1 - odd, c]
        far = got_out[odd, c]
        near_low, near_high = near[:HALO].astype(F32), near[HALO:].astype(F32)
        far_low, far_high = far[:HALO].astype(F32), far[HALO:].astype(F32)
        west.append(jnp.where(odd == 1, near_high, far_high))
        east.append(jnp.where(odd == 1, far_low, near_low))
        own.append(fields[c].astype(F32) if c < chans - 1 else mask[...].astype(F32))
    return west, own, east


def edge_kernel(columns, mask, metric, edges, halved):
    feeds = columns.shape[0]
    span_x = mask.shape[0]
    edges[:feeds] = columns[...]
    for part, start in enumerate((0, span_x - HALO)):
        edges[feeds, part * HALO : (part + 1) * HALO] = mask[start : start + HALO].astype(F32).astype(BF16)
    halved[...] = metric[...] * 0.5


def pack_kernel(fields, mask, got_in, got_out, pay_in, pay_out, own_low, own_top):
    chans = fields.shape[0] + 1
    span_x, span_y = mask.shape
    wide = span_x + 2 * HALO
    lat, last = lax.axis_index("gy"), lax.axis_size("gy") - 1
    odd = lax.rem(lat, 2) == 1
    west, own, east = sides(fields, mask, got_in, got_out)
    pad = jnp.zeros((span_y - wide, span_y), F32)
    slot = 4 * HALO
    lane = iota((wide, span_y), 1)
    low, top = [], []
    for first in range(0, chans, span_y // slot):
        group = range(first, min(first + span_y // slot, chans))
        gathered = jnp.zeros((wide, span_y), F32)
        for i, c in enumerate(group):
            col = jnp.concatenate([west[c], own[c], east[c]], axis=0)
            here = (lane >= i * slot) & (lane < (i + 1) * slot)
            gathered = jnp.where(here, turn(col, i * slot + 2 * HALO), gathered)
        turned = jnp.concatenate([gathered, pad], axis=0).T
        for i, c in enumerate(group):
            own_top[c] = turned[i * slot : i * slot + 2 * HALO]
            own_low[c] = turned[i * slot + 2 * HALO : (i + 1) * slot]
            top.append(turned[i * slot + HALO : i * slot + 2 * HALO])
            low.append(turned[i * slot + 2 * HALO : i * slot + 3 * HALO])
    low = jnp.concatenate(low, axis=0)
    top = jnp.concatenate(top, axis=0)
    a, b = iota((span_y, span_y), 0), iota((span_y, span_y), 1)
    flip_x = (a + b == wide - 1).astype(BF16)
    a, b = iota((chans * HALO, chans * HALO), 0), iota((chans * HALO, chans * HALO), 1)
    flip_y = ((a // HALO == b // HALO) & (a % HALO + b % HALO == HALO - 1)).astype(BF16)
    mirrored = jnp.dot(top.astype(BF16), flip_x, preferred_element_type=F32).astype(BF16)
    mirrored = jnp.dot(flip_y, mirrored, preferred_element_type=F32)
    out_top = jnp.where(lat == last, mirrored, top)
    for c in range(chans):
        part = slice(c * HALO, (c + 1) * HALO)
        pay_in[c] = jnp.where(odd, low[part], top[part]).astype(BF16)
        pay_out[c] = jnp.where(odd, out_top[part], low[part]).astype(BF16)


def ones_rows(lanes):
    return (iota((ONES, lanes), 0) < 3).astype(BF16)


def turn(v, by):
    return pltpu.roll(v, by % v.shape[-1], v.ndim - 1)


def first_taps(window, order):
    pieces = [[] for _ in range(5)]
    for w in window:
        west, here, east = w[:8], w[1:9], w[2:]
        pieces[0].append(turn(west, 1) + turn(east, -1))
        pieces[1].append(west + east)
        pieces[2].append(turn(west, -1) + turn(east, 1))
        pieces[3].append(turn(here, 1) + turn(here, -1))
        pieces[4].append(here)
    stacked = jnp.concatenate([p for t in order for p in pieces[t]], axis=0).astype(BF16)
    return jnp.concatenate([stacked, ones_rows(stacked.shape[1])], axis=0)


def hidden_taps(load, row, order):
    parts = [
        load(1, row - 1) + load(2, row + 1),
        load(0, row - 1) + load(0, row + 1),
        load(2, row - 1) + load(1, row + 1),
        load(1, row) + load(2, row),
        load(0, row),
    ]
    return jnp.concatenate([parts[t] for t in order] + [ones_rows(parts[0].shape[1])], axis=0)


def loader(src):
    seen = {}

    def load(version, row):
        if (version, row) not in seen:
            seen[version, row] = src[version, row]
        return seen[version, row]

    return load


def activate(summed, ocean_row):
    ocean = jnp.broadcast_to(ocean_row, (16, ocean_row.shape[1])).astype(BF16)
    ocean = jnp.concatenate([ocean] * (summed.shape[0] // 16), axis=0)
    return jnp.maximum(summed.astype(BF16), jnp.zeros((), BF16)) * ocean


def put(dst, row, v):
    dst[0, row] = v
    dst[1, row] = turn(v, 1)
    dst[2, row] = turn(v, -1)


def bias_columns(biases, k):
    hid = biases.shape[1]
    a, b = iota((hid, hid), 0), iota((hid, hid), 1)
    row = jnp.broadcast_to(biases[k : k + 1, :], (hid, hid))
    rest = jnp.sum(jnp.where(a == b, row, 0.0), axis=1, keepdims=True)
    spread = jnp.zeros((hid, ONES), F32)
    at = iota((hid, ONES), 1)
    for i in range(3):
        piece = rest.astype(BF16).astype(F32)
        spread = jnp.where(at == i, jnp.broadcast_to(piece, (hid, ONES)), spread)
        rest = rest - piece
    return spread


def arrange_weights(w_first, w_mid, w_last, biases, big, hidden, final):
    taps, feeds, hid = w_first.shape
    n_mid = w_mid.shape[0]
    depth = taps * feeds * 8
    final[...] = jnp.zeros_like(final)
    lanes = 128
    stacked = [w_first[t].astype(F32) for t in range(taps)]
    stacked = jnp.concatenate(stacked + [jnp.zeros((lanes - taps * feeds, hid), F32)], axis=0)
    stacked = jnp.concatenate([stacked, jnp.zeros((lanes, lanes - hid), F32)], axis=1).T
    a, b = iota((lanes, depth), 0), iota((lanes, depth), 1)
    place = (b // 8 == a).astype(BF16)
    spread = jnp.dot(stacked[:hid].astype(BF16), place, preferred_element_type=F32)
    for t in range(taps):
        final[: w_last.shape[1], t * hid : (t + 1) * hid] = w_last[t]
        for k in range(n_mid):
            hidden[k, :, t * hid : (t + 1) * hid] = w_mid[k, t]
    sub = iota((hid, depth), 1) % 8
    first_bias = bias_columns(biases, 0).astype(BF16)
    for r in range(8):
        big[r * hid : (r + 1) * hid, :depth] = jnp.where(sub == r, spread, 0.0).astype(BF16)
        big[r * hid : (r + 1) * hid, depth:] = first_bias
    for k in range(n_mid):
        hidden[k, :, taps * hid :] = bias_columns(biases, k + 1).astype(BF16)


def waits_long():
    place = lax.rem(lax.axis_index("gx"), lax.axis_size("gx") // 4)
    top = lax.axis_index("gy") == lax.axis_size("gy") - 1
    origin = (lax.axis_index("gx") == 0) & (lax.axis_index("gy") == 0)
    return jnp.logical_not(origin) & ((place == 0) | (top & (place < EARLY)))


def halves(v):
    half = v.shape[1] // 2
    return v[:, :half], v[:, half:]


def masked_stress(summed, ocean_row):
    return (summed[:8] * ocean_row).astype(BF16).astype(F32)


def inner_columns(fields, mask, w_first, w_mid, w_last, biases, stress, kept, big, hidden, final, ext, h_a, h_b):
    feeds, span_x, span_y = fields.shape
    n_mid = w_mid.shape[0]
    hid = w_first.shape[2]
    arrange_weights(w_first, w_mid, w_last, biases, big, hidden, final)
    for c in range(feeds):
        ext[c, :HALO] = jnp.zeros((HALO, span_y), F32)
        ext[c, HALO : HALO + span_x] = fields[c].astype(F32)
        ext[c, HALO + span_x :] = jnp.zeros((HALO, span_y), F32)
    ext[feeds, HALO : HALO + span_x] = mask[...].astype(F32)

    def ocean_row(row):
        return ext[feeds, HALO + row : HALO + row + 1, :]

    def keep(k, row, v):
        for slot, at in enumerate((k, k + 1, span_x - k - 2, span_x - k - 1)):
            if row == at:
                kept[k - 1, slot] = v

    for start in range(0, span_x, 16):
        taps = [
            first_taps([ext[c, HALO + row - 1 : HALO + row + 9, :] for c in range(feeds)], ALONG_X)
            for row in (start, start + 8)
        ]
        summed = jnp.dot(big[...], jnp.concatenate(taps, axis=1), preferred_element_type=F32)
        for part, row in zip(halves(summed), (start, start + 8)):
            for r in range(8):
                v = activate(part[r * hid : (r + 1) * hid], ocean_row(row + r))
                put(h_a, row + r, v)
                keep(1, row + r, v)

    def layer(weights, src, k, finish):
        cached = loader(src)
        for start in range(k, span_x - k, 2):
            taps = [hidden_taps(cached, row, ALONG_X) for row in (start, start + 1)]
            summed = jnp.dot(weights, jnp.concatenate(taps, axis=1), preferred_element_type=F32)
            for part, row in zip(halves(summed), (start, start + 1)):
                finish(part, row)

    src, dst = h_a, h_b
    for k in range(2, n_mid + 2):

        def finish(summed, row):
            v = activate(summed, ocean_row(row))
            put(dst, row, v)
            keep(k, row, v)

        layer(hidden[k - 2], src, k, finish)
        src, dst = dst, src

    def finish(summed, row):
        v = masked_stress(summed, ocean_row(row))
        for c in range(3):
            stress[c, HALO + row : HALO + row + 1, :] = v[c : c + 1]

    layer(final[...], src, n_mid + 2, finish)


def early_kernel(
    edges, got_in, fields, mask, w_first, w_mid, w_last, biases,
    edges_out, stress, kept, big, hidden, final, ext, h_a, h_b,
):
    del got_in
    edges_out[...] = edges[...]

    @pl.when(waits_long())
    def _():
        inner_columns(
            fields, mask, w_first, w_mid, w_last, biases, stress, kept, big, hidden, final, ext, h_a, h_b
        )


def late_kernel(
    fields, mask, w_first, w_mid, w_last, biases, stress_in, kept_in, big_in, hidden_in, final_in, lat_out,
    stress, kept, big, hidden, final, ext, h_a, h_b,
):
    del lat_out

    @pl.when(waits_long())
    def _():
        pairs = ((stress_in, stress), (kept_in, kept), (big_in, big), (hidden_in, hidden), (final_in, final))
        for done, here in pairs:
            here[...] = done[...]

    @pl.when(jnp.logical_not(waits_long()))
    def _():
        inner_columns(
            fields, mask, w_first, w_mid, w_last, biases, stress, kept, big, hidden, final, ext, h_a, h_b
        )


def side_layers(ext, kept, span_x, big, hidden, final, src, dst, stress):
    n_mid, hid, _ = hidden.shape
    feeds = ext.shape[0] - 1
    starts = (-6, span_x - 2)

    def places(k, slot):
        return k - 8 + slot, span_x - 2 - k + slot

    def ocean_row(row):
        return ext[feeds, HALO + row : HALO + row + 1, :]

    def fill(dst, k):
        for slot in range(2):
            put(dst.at[0], 8 + slot, kept[k - 1, slot])
            put(dst.at[1], slot, kept[k - 1, 2 + slot])

    taps = [
        first_taps([ext[c, HALO + row - 1 : HALO + row + 9, :] for c in range(feeds)], ALONG_X) for row in starts
    ]
    summed = jnp.dot(big[...], jnp.concatenate(taps, axis=1), preferred_element_type=F32)
    for side, part in enumerate(halves(summed)):
        for slot in range(2, 8):
            row = places(1, slot)[side]
            r = row - starts[side]
            put(src.at[side], slot, activate(part[r * hid : (r + 1) * hid], ocean_row(row)))
    fill(src, 1)
    yield
    for k in range(2, n_mid + 3):
        loads = [loader(src.at[side]) for side in range(2)]
        weights = hidden[k - 2] if k < n_mid + 2 else final[...]
        for slot in range(2, 8):
            taps = [hidden_taps(loads[0], slot + 1, ALONG_X), hidden_taps(loads[1], slot - 1, ALONG_X)]
            summed = jnp.dot(weights, jnp.concatenate(taps, axis=1), preferred_element_type=F32)
            for side, part in enumerate(halves(summed)):
                row = places(k, slot)[side]
                if k < n_mid + 2:
                    put(dst.at[side], slot, activate(part, ocean_row(row)))
                else:
                    v = masked_stress(part, ocean_row(row))
                    for c in range(3):
                        stress[c, HALO + row : HALO + row + 1, :] = v[c : c + 1]
            yield
        if k < n_mid + 2:
            fill(dst, k)
        src, dst = dst, src


def strip_layers(ext, span_y, big, hidden, final, src, dst, edge):
    n_mid, hid, _ = hidden.shape
    feeds = ext.shape[0] - 1

    def ocean_row(row):
        return ext[feeds, row : row + 1, :]

    def put_both(dst, row, v):
        for half in range(2):
            lanes = slice(half * span_y, (half + 1) * span_y)
            part = v[:, lanes]
            dst[0, row, :, lanes] = part
            dst[1, row, :, lanes] = turn(part, 1)
            dst[2, row, :, lanes] = turn(part, -1)

    for row in (8, 16):
        taps = [
            first_taps([ext[c, row - 1 : row + 9, half * span_y : (half + 1) * span_y] for c in range(feeds)], ALONG_Y)
            for half in range(2)
        ]
        summed = jnp.dot(big[...], jnp.concatenate(taps, axis=1), preferred_element_type=F32)
        for r in range(8):
            put_both(src, row + r, activate(summed[r * hid : (r + 1) * hid], ocean_row(row + r)))
        yield
    for k in range(n_mid):
        cached = loader(src)
        for row in range(10 + k, 22 - k):
            taps = hidden_taps(cached, row, ALONG_Y)
            summed = jnp.dot(hidden[k], taps, preferred_element_type=F32)
            put_both(dst, row, activate(summed, ocean_row(row)))
            if row % 2:
                yield
        src, dst = dst, src
    slot = 2 * HALO
    cached = loader(src)
    for row in range(13, 19):
        summed = jnp.dot(final[...], hidden_taps(cached, row, ALONG_Y), preferred_element_type=F32)
        v = masked_stress(summed, ocean_row(row))
        for c in range(3):
            edge[c * slot + row - 13 : c * slot + row - 12, :] = v[c : c + 1, :span_y]
            edge[c * slot + row - 5 : c * slot + row - 4, :] = v[c : c + 1, span_y:]
        if row % 2:
            yield


def edge_lines_kernel(
    fields, mask, got_in, got_out, own_low, own_top, lat_in, lat_out, stress_in, kept, big, hidden, final, halved, out,
    ext, ext_strip, rows_a, rows_b, h_a, h_b, stress, edge,
):
    feeds, span_x, span_y = fields.shape
    lat, last = lax.axis_index("gy"), lax.axis_size("gy") - 1
    odd = lax.rem(lat, 2) == 1
    lower = lax.axis_index("gx") < lax.axis_size("gx") // 2
    partner = jnp.where(jnp.where(lat == last, lower, odd), 1, 0)
    stress[...] = stress_in[...]
    west, own, east = sides(fields, mask, got_in, got_out)
    for c in range(feeds + 1):
        ext[c, :HALO] = west[c]
        ext[c, HALO : HALO + span_x] = own[c]
        ext[c, HALO + span_x :] = east[c]
    ext_strip[...] = jnp.zeros_like(ext_strip)
    for c in range(feeds + 1):
        inner = lat_in[c].astype(F32)
        outer = lat_out[partner, c].astype(F32)
        outer = jnp.where(lat == 0, jnp.zeros_like(outer), outer)
        below = jnp.where(odd, inner, outer)
        above = jnp.where(odd, outer, inner)
        ext_strip[c, 6:14, :span_y] = below
        ext_strip[c, 14:30, :span_y] = own_low[c]
        ext_strip[c, 2:18, span_y:] = own_top[c]
        ext_strip[c, 18:26, span_y:] = above

    todo = [
        strip_layers(ext_strip, span_y, big, hidden, final, h_a, h_b, edge),
        side_layers(ext, kept, span_x, big, hidden, final, rows_a, rows_b, stress),
    ]
    while todo:
        todo = [layers for layers in todo if next(layers, todo) is None]

    slot = 2 * HALO
    turned = edge[...].T[HALO - 1 : HALO + span_x + 1]

    half_x = halved[0:1, :]
    half_y = halved[1:2, :]
    ocean = mask[...].astype(F32)
    lane = iota((span_x + 2, span_y), 1)
    inner = lane[:span_x]
    planes, north, south = [], [], []
    for c in range(3):
        low = turn(turned, -(c * slot + 1))
        high = turn(turned, span_y - 5 - (c * slot + HALO))
        plane = jnp.where(lane < 5, low, jnp.where(lane >= span_y - 5, high, stress[c, HALO - 1 : HALO + span_x + 1, :]))
        here = plane[1 : 1 + span_x]
        beyond = turn(turned[1 : 1 + span_x], span_y - 1 - (c * slot + HALO + 5))
        below = turn(turned[1 : 1 + span_x], -c * slot)
        planes.append(plane)
        north.append(jnp.where(inner == span_y - 1, beyond, turn(here, -1)))
        south.append(jnp.where(inner == 0, below, turn(here, 1)))

    def diff_x(c):
        return (planes[c][2:] - planes[c][:span_x]) * half_x

    def diff_y(c):
        return (north[c] - south[c]) * half_y

    out[0] = (diff_x(0) + diff_y(1)) * ocean
    out[1] = (diff_x(1) + diff_y(2)) * ocean


def pack(fields, mask, got_in, got_out):
    chans, span_y = fields.shape[0] + 1, mask.shape[1]
    return pl.pallas_call(
        pack_kernel,
        out_shape=[jax.ShapeDtypeStruct((chans, HALO, span_y), BF16)] * 2
        + [jax.ShapeDtypeStruct((chans, 2 * HALO, span_y), F32)] * 2,
        in_specs=[VMEM] * 4,
        out_specs=[VMEM] * 4,
        compiler_params=pltpu.CompilerParams(vmem_limit_bytes=4 * 1024 * 1024),
        name="pack_rows",
    )(fields, mask, got_in, got_out)


def outermost(fields, mask, metric):
    feeds, span_x, span_y = fields.shape
    columns = jnp.concatenate([fields[:, :HALO], fields[:, span_x - HALO :]], axis=1)
    return pl.pallas_call(
        edge_kernel,
        out_shape=[
            jax.ShapeDtypeStruct((feeds + 1, 2 * HALO, span_y), BF16),
            jax.ShapeDtypeStruct(metric.shape, F32),
        ],
        in_specs=[VMEM] * 3,
        out_specs=[VMEM] * 2,
        compiler_params=pltpu.CompilerParams(vmem_limit_bytes=4 * 1024 * 1024),
        cost_estimate=pl.CostEstimate(flops=10_000_000_000, bytes_accessed=1_000_000, transcendentals=0),
        name="outermost_columns",
    )(columns, mask, metric)


def inner_shapes(fields, w_first, w_mid):
    feeds, span_x, span_y = fields.shape
    taps, _, hid = w_first.shape
    n_mid = w_mid.shape[0]
    rows = span_x + 2 * HALO
    outs = [
        jax.ShapeDtypeStruct((3, rows, span_y), F32),
        jax.ShapeDtypeStruct((n_mid + 1, 4, hid, span_y), BF16),
        jax.ShapeDtypeStruct((8 * hid, taps * feeds * 8 + ONES), BF16),
        jax.ShapeDtypeStruct((n_mid, hid, taps * hid + ONES), BF16),
        jax.ShapeDtypeStruct((16, taps * hid + ONES), BF16),
    ]
    scratch = [
        pltpu.VMEM((feeds + 1, rows, span_y), F32),
        pltpu.VMEM((3, span_x, hid, span_y), BF16),
        pltpu.VMEM((3, span_x, hid, span_y), BF16),
    ]
    return outs, scratch


def early(edges, got_in, fields, mask, w_first, w_mid, w_last, biases):
    outs, scratch = inner_shapes(fields, w_first, w_mid)
    return pl.pallas_call(
        early_kernel,
        out_shape=[jax.ShapeDtypeStruct(edges.shape, edges.dtype)] + outs,
        in_specs=[VMEM] * 8,
        out_specs=[VMEM] * 6,
        scratch_shapes=scratch,
        compiler_params=pltpu.CompilerParams(vmem_limit_bytes=12 * 1024 * 1024),
        name="inner_early",
    )(edges, got_in, fields, mask, w_first, w_mid, w_last, biases)


def late(fields, mask, w_first, w_mid, w_last, biases, done, lat_out):
    outs, scratch = inner_shapes(fields, w_first, w_mid)
    return pl.pallas_call(
        late_kernel,
        out_shape=outs,
        in_specs=[VMEM] * 12,
        out_specs=[VMEM] * 5,
        scratch_shapes=scratch,
        compiler_params=pltpu.CompilerParams(vmem_limit_bytes=12 * 1024 * 1024),
        cost_estimate=pl.CostEstimate(flops=5_000_000_000, bytes_accessed=20_000_000, transcendentals=0),
        name="inner_late",
    )(fields, mask, w_first, w_mid, w_last, biases, *done, lat_out)


def edge_lines(fields, mask, got_in, got_out, own_low, own_top, lat_in, lat_out, inner, halved):
    feeds, span_x, span_y = fields.shape
    stress, _, _, hidden, _ = inner
    hid = hidden.shape[1]
    return pl.pallas_call(
        edge_lines_kernel,
        out_shape=jax.ShapeDtypeStruct((2, span_x, span_y), F32),
        in_specs=[VMEM] * 14,
        out_specs=VMEM,
        scratch_shapes=[
            pltpu.VMEM((feeds + 1, span_x + 2 * HALO, span_y), F32),
            pltpu.VMEM((feeds + 1, STRIP, 2 * span_y), F32),
            pltpu.VMEM((2, 3, 10, hid, span_y), BF16),
            pltpu.VMEM((2, 3, 10, hid, span_y), BF16),
            pltpu.VMEM((3, STRIP, hid, 2 * span_y), BF16),
            pltpu.VMEM((3, STRIP, hid, 2 * span_y), BF16),
            pltpu.VMEM(stress.shape, F32),
            pltpu.VMEM((span_y, span_y), F32),
        ],
        compiler_params=pltpu.CompilerParams(vmem_limit_bytes=12 * 1024 * 1024),
        name="edge_lines",
    )(fields, mask, got_in, got_out, own_low, own_top, lat_in, lat_out, *inner, halved)


def latitude_swaps(count_x, count_y):
    at = lambda g, y: g * count_y + y
    up = [(at(g, y), at(g, y + 1)) for g in range(count_x) for y in range(0, count_y, 2)]
    return up + [(target, source) for source, target in up]


def latitude_groups(count_x, count_y):
    at = lambda g, y: g * count_y + y
    pairs = [[at(g, y), at(g, y + 1)] for g in range(count_x) for y in range(1, count_y - 1, 2)]
    pairs += [[at(g, count_y - 1), at(count_x - 1 - g, count_y - 1)] for g in range(count_x // 2)]
    return pairs + [[at(g, 0), at((g + 1) % count_x, 0)] for g in range(1, count_x, 2)]


def on_device(fields, ocean_mask, metric, w_first, w_mid, w_last, biases):
    count_x, count_y = lax.axis_size("gx"), lax.axis_size("gy")
    inside = [[i, i + 1] for i in range(0, count_x, 2)]
    across = [[i, (i + 1) % count_x] for i in range(1, count_x, 2)]
    weights = (jnp.swapaxes(w_first, 1, 2), w_mid, w_last, biases)
    edges, halved = outermost(fields, ocean_mask, metric)
    got_in = lax.all_gather(edges, "gx", axis_index_groups=inside)
    edges, *done = early(edges, got_in, fields, ocean_mask, *weights)
    got_out = lax.all_gather(edges, "gx", axis_index_groups=across)
    pay_in, pay_out, own_low, own_top = pack(fields, ocean_mask, got_in, got_out)
    lat_in = lax.ppermute(pay_in, ("gx", "gy"), latitude_swaps(count_x, count_y))
    lat_out = lax.all_gather(pay_out, ("gx", "gy"), axis_index_groups=latitude_groups(count_x, count_y))
    inner = late(fields, ocean_mask, *weights, done, lat_out)
    return edge_lines(fields, ocean_mask, got_in, got_out, own_low, own_top, lat_in, lat_out, inner, halved)


def solution(mesh):
    placed = (P(None, "gx", "gy"), P("gx", "gy"), P(None, "gy"), P(), P(), P(), P())
    return jax.shard_map(
        on_device, mesh=mesh, in_specs=placed, out_specs=P(None, "gx", "gy"), check_vma=False
    )
```

```python
import jax
import jax.numpy as jnp
from jax import lax
from jax.experimental import pallas as pl
from jax.experimental.pallas import tpu as pltpu
from jax.sharding import PartitionSpec as P

HALO = 8
EARLY = 8
ONES = 16
STRIP = 32
F32 = jnp.float32
BF16 = jnp.bfloat16
ALONG_X = (0, 1, 2, 3, 4)
ALONG_Y = (0, 3, 2, 1, 4)
VMEM = pl.BlockSpec(memory_space=pltpu.VMEM)


def iota(shape, dim):
    return lax.broadcasted_iota(jnp.int32, shape, dim)


def sides(fields, mask, got_in, got_out):
    chans = fields.shape[0] + 1
    odd = lax.rem(lax.axis_index("gx"), 2)
    west, own, east = [], [], []
    for c in range(chans):
        near = got_in[1 - odd, c]
        far = got_out[odd, c]
        near_low, near_high = near[:HALO].astype(F32), near[HALO:].astype(F32)
        far_low, far_high = far[:HALO].astype(F32), far[HALO:].astype(F32)
        west.append(jnp.where(odd == 1, near_high, far_high))
        east.append(jnp.where(odd == 1, far_low, near_low))
        own.append(fields[c].astype(F32) if c < chans - 1 else mask[...].astype(F32))
    return west, own, east


def edge_kernel(columns, mask, metric, edges, halved):
    feeds = columns.shape[0]
    span_x = mask.shape[0]
    edges[:feeds] = columns[...]
    for part, start in enumerate((0, span_x - HALO)):
        edges[feeds, part * HALO : (part + 1) * HALO] = mask[start : start + HALO].astype(F32).astype(BF16)
    halved[...] = metric[...] * 0.5


def pack_kernel(fields, mask, got_in, got_out, pay_in, pay_out, own_low, own_top):
    chans = fields.shape[0] + 1
    span_x, span_y = mask.shape
    wide = span_x + 2 * HALO
    lat, last = lax.axis_index("gy"), lax.axis_size("gy") - 1
    odd = lax.rem(lat, 2) == 1
    west, own, east = sides(fields, mask, got_in, got_out)
    pad = jnp.zeros((span_y - wide, span_y), F32)
    slot = 4 * HALO
    lane = iota((wide, span_y), 1)
    low, top = [], []
    for first in range(0, chans, span_y // slot):
        group = range(first, min(first + span_y // slot, chans))
        gathered = jnp.zeros((wide, span_y), F32)
        for i, c in enumerate(group):
            col = jnp.concatenate([west[c], own[c], east[c]], axis=0)
            here = (lane >= i * slot) & (lane < (i + 1) * slot)
            gathered = jnp.where(here, turn(col, i * slot + 2 * HALO), gathered)
        turned = jnp.concatenate([gathered, pad], axis=0).T
        for i, c in enumerate(group):
            own_top[c] = turned[i * slot : i * slot + 2 * HALO]
            own_low[c] = turned[i * slot + 2 * HALO : (i + 1) * slot]
            top.append(turned[i * slot + HALO : i * slot + 2 * HALO])
            low.append(turned[i * slot + 2 * HALO : i * slot + 3 * HALO])
    low = jnp.concatenate(low, axis=0)
    top = jnp.concatenate(top, axis=0)
    a, b = iota((span_y, span_y), 0), iota((span_y, span_y), 1)
    flip_x = (a + b == wide - 1).astype(BF16)
    a, b = iota((chans * HALO, chans * HALO), 0), iota((chans * HALO, chans * HALO), 1)
    flip_y = ((a // HALO == b // HALO) & (a % HALO + b % HALO == HALO - 1)).astype(BF16)
    mirrored = jnp.dot(top.astype(BF16), flip_x, preferred_element_type=F32).astype(BF16)
    mirrored = jnp.dot(flip_y, mirrored, preferred_element_type=F32)
    out_top = jnp.where(lat == last, mirrored, top)
    for c in range(chans):
        part = slice(c * HALO, (c + 1) * HALO)
        pay_in[c] = jnp.where(odd, low[part], top[part]).astype(BF16)
        pay_out[c] = jnp.where(odd, out_top[part], low[part]).astype(BF16)


def ones_rows(lanes):
    return (iota((ONES, lanes), 0) < 3).astype(BF16)


def turn(v, by):
    return pltpu.roll(v, by % v.shape[-1], v.ndim - 1)


def first_taps(window, order):
    pieces = [[] for _ in range(5)]
    for w in window:
        west, here, east = w[:8], w[1:9], w[2:]
        pieces[0].append(turn(west, 1) + turn(east, -1))
        pieces[1].append(west + east)
        pieces[2].append(turn(west, -1) + turn(east, 1))
        pieces[3].append(turn(here, 1) + turn(here, -1))
        pieces[4].append(here)
    stacked = jnp.concatenate([p for t in order for p in pieces[t]], axis=0).astype(BF16)
    return jnp.concatenate([stacked, ones_rows(stacked.shape[1])], axis=0)


def hidden_taps(load, row, order):
    parts = [
        load(1, row - 1) + load(2, row + 1),
        load(0, row - 1) + load(0, row + 1),
        load(2, row - 1) + load(1, row + 1),
        load(1, row) + load(2, row),
        load(0, row),
    ]
    return jnp.concatenate([parts[t] for t in order] + [ones_rows(parts[0].shape[1])], axis=0)


def loader(src):
    seen = {}

    def load(version, row):
        if (version, row) not in seen:
            seen[version, row] = src[version, row]
        return seen[version, row]

    return load


def activate(summed, ocean_row):
    ocean = jnp.broadcast_to(ocean_row, (16, ocean_row.shape[1])).astype(BF16)
    ocean = jnp.concatenate([ocean] * (summed.shape[0] // 16), axis=0)
    return jnp.maximum(summed.astype(BF16), jnp.zeros((), BF16)) * ocean


def put(dst, row, v):
    dst[0, row] = v
    dst[1, row] = turn(v, 1)
    dst[2, row] = turn(v, -1)


def bias_columns(biases, k):
    hid = biases.shape[1]
    a, b = iota((hid, hid), 0), iota((hid, hid), 1)
    row = jnp.broadcast_to(biases[k : k + 1, :], (hid, hid))
    rest = jnp.sum(jnp.where(a == b, row, 0.0), axis=1, keepdims=True)
    spread = jnp.zeros((hid, ONES), F32)
    at = iota((hid, ONES), 1)
    for i in range(3):
        piece = rest.astype(BF16).astype(F32)
        spread = jnp.where(at == i, jnp.broadcast_to(piece, (hid, ONES)), spread)
        rest = rest - piece
    return spread


def arrange_weights(w_first, w_mid, w_last, biases, big, hidden, final):
    taps, feeds, hid = w_first.shape
    n_mid = w_mid.shape[0]
    depth = taps * feeds * 8
    final[...] = jnp.zeros_like(final)
    lanes = 128
    stacked = [w_first[t].astype(F32) for t in range(taps)]
    stacked = jnp.concatenate(stacked + [jnp.zeros((lanes - taps * feeds, hid), F32)], axis=0)
    stacked = jnp.concatenate([stacked, jnp.zeros((lanes, lanes - hid), F32)], axis=1).T
    a, b = iota((lanes, depth), 0), iota((lanes, depth), 1)
    place = (b // 8 == a).astype(BF16)
    spread = jnp.dot(stacked[:hid].astype(BF16), place, preferred_element_type=F32)
    for t in range(taps):
        final[: w_last.shape[1], t * hid : (t + 1) * hid] = w_last[t]
        for k in range(n_mid):
            hidden[k, :, t * hid : (t + 1) * hid] = w_mid[k, t]
    sub = iota((hid, depth), 1) % 8
    first_bias = bias_columns(biases, 0).astype(BF16)
    for r in range(8):
        big[r * hid : (r + 1) * hid, :depth] = jnp.where(sub == r, spread, 0.0).astype(BF16)
        big[r * hid : (r + 1) * hid, depth:] = first_bias
    for k in range(n_mid):
        hidden[k, :, taps * hid :] = bias_columns(biases, k + 1).astype(BF16)


def waits_long():
    place = lax.rem(lax.axis_index("gx"), lax.axis_size("gx") // 4)
    top = lax.axis_index("gy") == lax.axis_size("gy") - 1
    origin = (lax.axis_index("gx") == 0) & (lax.axis_index("gy") == 0)
    return jnp.logical_not(origin) & ((place == 0) | (top & (place < EARLY)))


def halves(v):
    half = v.shape[1] // 2
    return v[:, :half], v[:, half:]


def masked_stress(summed, ocean_row):
    return (summed[:8] * ocean_row).astype(BF16).astype(F32)


def inner_columns(fields, mask, w_first, w_mid, w_last, biases, stress, kept, big, hidden, final, ext, h_a, h_b):
    feeds, span_x, span_y = fields.shape
    n_mid = w_mid.shape[0]
    hid = w_first.shape[2]
    arrange_weights(w_first, w_mid, w_last, biases, big, hidden, final)
    for c in range(feeds):
        ext[c, :HALO] = jnp.zeros((HALO, span_y), F32)
        ext[c, HALO : HALO + span_x] = fields[c].astype(F32)
        ext[c, HALO + span_x :] = jnp.zeros((HALO, span_y), F32)
    ext[feeds, HALO : HALO + span_x] = mask[...].astype(F32)

    def ocean_row(row):
        return ext[feeds, HALO + row : HALO + row + 1, :]

    def keep(k, row, v):
        for slot, at in enumerate((k, k + 1, span_x - k - 2, span_x - k - 1)):
            if row == at:
                kept[k - 1, slot] = v

    for start in range(0, span_x, 16):
        taps = [
            first_taps([ext[c, HALO + row - 1 : HALO + row + 9, :] for c in range(feeds)], ALONG_X)
            for row in (start, start + 8)
        ]
        summed = jnp.dot(big[...], jnp.concatenate(taps, axis=1), preferred_element_type=F32)
        for part, row in zip(halves(summed), (start, start + 8)):
            for r in range(8):
                v = activate(part[r * hid : (r + 1) * hid], ocean_row(row + r))
                put(h_a, row + r, v)
                keep(1, row + r, v)

    def layer(weights, src, k, finish):
        cached = loader(src)
        for start in range(k, span_x - k, 2):
            taps = [hidden_taps(cached, row, ALONG_X) for row in (start, start + 1)]
            summed = jnp.dot(weights, jnp.concatenate(taps, axis=1), preferred_element_type=F32)
            for part, row in zip(halves(summed), (start, start + 1)):
                finish(part, row)

    src, dst = h_a, h_b
    for k in range(2, n_mid + 2):

        def finish(summed, row):
            v = activate(summed, ocean_row(row))
            put(dst, row, v)
            keep(k, row, v)

        layer(hidden[k - 2], src, k, finish)
        src, dst = dst, src

    def finish(summed, row):
        v = masked_stress(summed, ocean_row(row))
        for c in range(3):
            stress[c, HALO + row : HALO + row + 1, :] = v[c : c + 1]

    layer(final[...], src, n_mid + 2, finish)


def early_kernel(
    edges, got_in, fields, mask, w_first, w_mid, w_last, biases,
    edges_out, stress, kept, big, hidden, final, ext, h_a, h_b,
):
    del got_in
    edges_out[...] = edges[...]

    @pl.when(waits_long())
    def _():
        inner_columns(
            fields, mask, w_first, w_mid, w_last, biases, stress, kept, big, hidden, final, ext, h_a, h_b
        )


def late_kernel(
    fields, mask, w_first, w_mid, w_last, biases, stress_in, kept_in, big_in, hidden_in, final_in, lat_out,
    stress, kept, big, hidden, final, ext, h_a, h_b,
):
    del lat_out

    @pl.when(waits_long())
    def _():
        pairs = ((stress_in, stress), (kept_in, kept), (big_in, big), (hidden_in, hidden), (final_in, final))
        for done, here in pairs:
            here[...] = done[...]

    @pl.when(jnp.logical_not(waits_long()))
    def _():
        inner_columns(
            fields, mask, w_first, w_mid, w_last, biases, stress, kept, big, hidden, final, ext, h_a, h_b
        )


def side_layers(ext, kept, span_x, big, hidden, final, src, dst, stress):
    n_mid, hid, _ = hidden.shape
    feeds = ext.shape[0] - 1
    starts = (-6, span_x - 2)

    def places(k, slot):
        return k - 8 + slot, span_x - 2 - k + slot

    def ocean_row(row):
        return ext[feeds, HALO + row : HALO + row + 1, :]

    def fill(dst, k):
        for slot in range(2):
            put(dst.at[0], 8 + slot, kept[k - 1, slot])
            put(dst.at[1], slot, kept[k - 1, 2 + slot])

    taps = [
        first_taps([ext[c, HALO + row - 1 : HALO + row + 9, :] for c in range(feeds)], ALONG_X) for row in starts
    ]
    summed = jnp.dot(big[...], jnp.concatenate(taps, axis=1), preferred_element_type=F32)
    for side, part in enumerate(halves(summed)):
        for slot in range(2, 8):
            row = places(1, slot)[side]
            r = row - starts[side]
            put(src.at[side], slot, activate(part[r * hid : (r + 1) * hid], ocean_row(row)))
    fill(src, 1)
    yield
    for k in range(2, n_mid + 3):
        loads = [loader(src.at[side]) for side in range(2)]
        weights = hidden[k - 2] if k < n_mid + 2 else final[...]
        for slot in range(2, 8):
            taps = [hidden_taps(loads[0], slot + 1, ALONG_X), hidden_taps(loads[1], slot - 1, ALONG_X)]
            summed = jnp.dot(weights, jnp.concatenate(taps, axis=1), preferred_element_type=F32)
            for side, part in enumerate(halves(summed)):
                row = places(k, slot)[side]
                if k < n_mid + 2:
                    put(dst.at[side], slot, activate(part, ocean_row(row)))
                else:
                    v = masked_stress(part, ocean_row(row))
                    for c in range(3):
                        stress[c, HALO + row : HALO + row + 1, :] = v[c : c + 1]
        yield
        if k < n_mid + 2:
            fill(dst, k)
        src, dst = dst, src


def strip_layers(ext, span_y, big, hidden, final, src, dst, edge):
    n_mid, hid, _ = hidden.shape
    feeds = ext.shape[0] - 1

    def ocean_row(row):
        return ext[feeds, row : row + 1, :]

    def put_both(dst, row, v):
        for half in range(2):
            lanes = slice(half * span_y, (half + 1) * span_y)
            part = v[:, lanes]
            dst[0, row, :, lanes] = part
            dst[1, row, :, lanes] = turn(part, 1)
            dst[2, row, :, lanes] = turn(part, -1)

    for row in (8, 16):
        taps = [
            first_taps([ext[c, row - 1 : row + 9, half * span_y : (half + 1) * span_y] for c in range(feeds)], ALONG_Y)
            for half in range(2)
        ]
        summed = jnp.dot(big[...], jnp.concatenate(taps, axis=1), preferred_element_type=F32)
        for r in range(8):
            put_both(src, row + r, activate(summed[r * hid : (r + 1) * hid], ocean_row(row + r)))
        yield
    for k in range(n_mid):
        cached = loader(src)
        for row in range(10 + k, 22 - k):
            taps = hidden_taps(cached, row, ALONG_Y)
            summed = jnp.dot(hidden[k], taps, preferred_element_type=F32)
            put_both(dst, row, activate(summed, ocean_row(row)))
        yield
        src, dst = dst, src
    slot = 2 * HALO
    cached = loader(src)
    for row in range(13, 19):
        summed = jnp.dot(final[...], hidden_taps(cached, row, ALONG_Y), preferred_element_type=F32)
        v = masked_stress(summed, ocean_row(row))
        for c in range(3):
            edge[c * slot + row - 13 : c * slot + row - 12, :] = v[c : c + 1, :span_y]
            edge[c * slot + row - 5 : c * slot + row - 4, :] = v[c : c + 1, span_y:]
        if row % 2:
            yield


def edge_lines_kernel(
    fields, mask, got_in, got_out, own_low, own_top, lat_in, lat_out, stress_in, kept, big, hidden, final, halved, out,
    ext, ext_strip, rows_a, rows_b, h_a, h_b, stress, edge,
):
    feeds, span_x, span_y = fields.shape
    lat, last = lax.axis_index("gy"), lax.axis_size("gy") - 1
    odd = lax.rem(lat, 2) == 1
    lower = lax.axis_index("gx") < lax.axis_size("gx") // 2
    partner = jnp.where(jnp.where(lat == last, lower, odd), 1, 0)
    stress[...] = stress_in[...]
    west, own, east = sides(fields, mask, got_in, got_out)
    for c in range(feeds + 1):
        ext[c, :HALO] = west[c]
        ext[c, HALO : HALO + span_x] = own[c]
        ext[c, HALO + span_x :] = east[c]
    for c in range(feeds + 1):
        inner = lat_in[c].astype(F32)
        outer = lat_out[partner, c].astype(F32)
        outer = jnp.where(lat == 0, jnp.zeros_like(outer), outer)
        below = jnp.where(odd, inner, outer)
        above = jnp.where(odd, outer, inner)
        ext_strip[c, 6:14, :span_y] = below
        ext_strip[c, 14:30, :span_y] = own_low[c]
        ext_strip[c, 2:18, span_y:] = own_top[c]
        ext_strip[c, 18:26, span_y:] = above

    todo = [
        strip_layers(ext_strip, span_y, big, hidden, final, h_a, h_b, edge),
        side_layers(ext, kept, span_x, big, hidden, final, rows_a, rows_b, stress),
    ]
    while todo:
        todo = [layers for layers in todo if next(layers, todo) is None]

    slot = 2 * HALO
    turned = edge[...].T[HALO - 1 : HALO + span_x + 1]

    half_x = halved[0:1, :]
    half_y = halved[1:2, :]
    ocean = mask[...].astype(F32)
    lane = iota((span_x + 2, span_y), 1)
    inner = lane[:span_x]
    planes, north, south = [], [], []
    for c in range(3):
        low = turn(turned, -(c * slot + 1))
        high = turn(turned, span_y - 5 - (c * slot + HALO))
        plane = jnp.where(lane < 5, low, jnp.where(lane >= span_y - 5, high, stress[c, HALO - 1 : HALO + span_x + 1, :]))
        here = plane[1 : 1 + span_x]
        beyond = turn(turned[1 : 1 + span_x], span_y - 1 - (c * slot + HALO + 5))
        below = turn(turned[1 : 1 + span_x], -c * slot)
        planes.append(plane)
        north.append(jnp.where(inner == span_y - 1, beyond, turn(here, -1)))
        south.append(jnp.where(inner == 0, below, turn(here, 1)))

    def diff_x(c):
        return (planes[c][2:] - planes[c][:span_x]) * half_x

    def diff_y(c):
        return (north[c] - south[c]) * half_y

    out[0] = (diff_x(0) + diff_y(1)) * ocean
    out[1] = (diff_x(1) + diff_y(2)) * ocean


def pack(fields, mask, got_in, got_out):
    chans, span_y = fields.shape[0] + 1, mask.shape[1]
    return pl.pallas_call(
        pack_kernel,
        out_shape=[jax.ShapeDtypeStruct((chans, HALO, span_y), BF16)] * 2
        + [jax.ShapeDtypeStruct((chans, 2 * HALO, span_y), F32)] * 2,
        in_specs=[VMEM] * 4,
        out_specs=[VMEM] * 4,
        compiler_params=pltpu.CompilerParams(vmem_limit_bytes=4 * 1024 * 1024),
        name="pack_rows",
    )(fields, mask, got_in, got_out)


def outermost(fields, mask, metric):
    feeds, span_x, span_y = fields.shape
    columns = jnp.concatenate([fields[:, :HALO], fields[:, span_x - HALO :]], axis=1)
    return pl.pallas_call(
        edge_kernel,
        out_shape=[
            jax.ShapeDtypeStruct((feeds + 1, 2 * HALO, span_y), BF16),
            jax.ShapeDtypeStruct(metric.shape, F32),
        ],
        in_specs=[VMEM] * 3,
        out_specs=[VMEM] * 2,
        compiler_params=pltpu.CompilerParams(vmem_limit_bytes=4 * 1024 * 1024),
        cost_estimate=pl.CostEstimate(flops=10_000_000_000, bytes_accessed=1_000_000, transcendentals=0),
        name="outermost_columns",
    )(columns, mask, metric)


def inner_shapes(fields, w_first, w_mid):
    feeds, span_x, span_y = fields.shape
    taps, _, hid = w_first.shape
    n_mid = w_mid.shape[0]
    rows = span_x + 2 * HALO
    outs = [
        jax.ShapeDtypeStruct((3, rows, span_y), F32),
        jax.ShapeDtypeStruct((n_mid + 1, 4, hid, span_y), BF16),
        jax.ShapeDtypeStruct((8 * hid, taps * feeds * 8 + ONES), BF16),
        jax.ShapeDtypeStruct((n_mid, hid, taps * hid + ONES), BF16),
        jax.ShapeDtypeStruct((16, taps * hid + ONES), BF16),
    ]
    scratch = [
        pltpu.VMEM((feeds + 1, rows, span_y), F32),
        pltpu.VMEM((3, span_x, hid, span_y), BF16),
        pltpu.VMEM((3, span_x, hid, span_y), BF16),
    ]
    return outs, scratch


def early(edges, got_in, fields, mask, w_first, w_mid, w_last, biases):
    outs, scratch = inner_shapes(fields, w_first, w_mid)
    return pl.pallas_call(
        early_kernel,
        out_shape=[jax.ShapeDtypeStruct(edges.shape, edges.dtype)] + outs,
        in_specs=[VMEM] * 8,
        out_specs=[VMEM] * 6,
        scratch_shapes=scratch,
        compiler_params=pltpu.CompilerParams(vmem_limit_bytes=12 * 1024 * 1024),
        name="inner_early",
    )(edges, got_in, fields, mask, w_first, w_mid, w_last, biases)


def late(fields, mask, w_first, w_mid, w_last, biases, done, lat_out):
    outs, scratch = inner_shapes(fields, w_first, w_mid)
    return pl.pallas_call(
        late_kernel,
        out_shape=outs,
        in_specs=[VMEM] * 12,
        out_specs=[VMEM] * 5,
        scratch_shapes=scratch,
        compiler_params=pltpu.CompilerParams(vmem_limit_bytes=12 * 1024 * 1024),
        cost_estimate=pl.CostEstimate(flops=5_000_000_000, bytes_accessed=20_000_000, transcendentals=0),
        name="inner_late",
    )(fields, mask, w_first, w_mid, w_last, biases, *done, lat_out)


def edge_lines(fields, mask, got_in, got_out, own_low, own_top, lat_in, lat_out, inner, halved):
    feeds, span_x, span_y = fields.shape
    stress, _, _, hidden, _ = inner
    hid = hidden.shape[1]
    return pl.pallas_call(
        edge_lines_kernel,
        out_shape=jax.ShapeDtypeStruct((2, span_x, span_y), F32),
        in_specs=[VMEM] * 14,
        out_specs=VMEM,
        scratch_shapes=[
            pltpu.VMEM((feeds + 1, span_x + 2 * HALO, span_y), F32),
            pltpu.VMEM((feeds + 1, STRIP, 2 * span_y), F32),
            pltpu.VMEM((2, 3, 10, hid, span_y), BF16),
            pltpu.VMEM((2, 3, 10, hid, span_y), BF16),
            pltpu.VMEM((3, STRIP, hid, 2 * span_y), BF16),
            pltpu.VMEM((3, STRIP, hid, 2 * span_y), BF16),
            pltpu.VMEM(stress.shape, F32),
            pltpu.VMEM((span_y, span_y), F32),
        ],
        compiler_params=pltpu.CompilerParams(vmem_limit_bytes=12 * 1024 * 1024),
        name="edge_lines",
    )(fields, mask, got_in, got_out, own_low, own_top, lat_in, lat_out, *inner, halved)


def latitude_swaps(count_x, count_y):
    at = lambda g, y: g * count_y + y
    up = [(at(g, y), at(g, y + 1)) for g in range(count_x) for y in range(0, count_y, 2)]
    return up + [(target, source) for source, target in up]


def latitude_groups(count_x, count_y):
    at = lambda g, y: g * count_y + y
    pairs = [[at(g, y), at(g, y + 1)] for g in range(count_x) for y in range(1, count_y - 1, 2)]
    pairs += [[at(g, count_y - 1), at(count_x - 1 - g, count_y - 1)] for g in range(count_x // 2)]
    return pairs + [[at(g, 0), at((g + 1) % count_x, 0)] for g in range(1, count_x, 2)]


def on_device(fields, ocean_mask, metric, w_first, w_mid, w_last, biases):
    count_x, count_y = lax.axis_size("gx"), lax.axis_size("gy")
    inside = [[i, i + 1] for i in range(0, count_x, 2)]
    across = [[i, (i + 1) % count_x] for i in range(1, count_x, 2)]
    weights = (jnp.swapaxes(w_first, 1, 2), w_mid, w_last, biases)
    edges, halved = outermost(fields, ocean_mask, metric)
    got_in = lax.all_gather(edges, "gx", axis_index_groups=inside)
    edges, *done = early(edges, got_in, fields, ocean_mask, *weights)
    got_out = lax.all_gather(edges, "gx", axis_index_groups=across)
    pay_in, pay_out, own_low, own_top = pack(fields, ocean_mask, got_in, got_out)
    lat_in = lax.ppermute(pay_in, ("gx", "gy"), latitude_swaps(count_x, count_y))
    lat_out = lax.all_gather(pay_out, ("gx", "gy"), axis_index_groups=latitude_groups(count_x, count_y))
    inner = late(fields, ocean_mask, *weights, done, lat_out)
    return edge_lines(fields, ocean_mask, got_in, got_out, own_low, own_top, lat_in, lat_out, inner, halved)


def solution(mesh):
    placed = (P(None, "gx", "gy"), P("gx", "gy"), P(None, "gy"), P(), P(), P(), P())
    return jax.shard_map(
        on_device, mesh=mesh, in_specs=placed, out_specs=P(None, "gx", "gy"), check_vma=False
    )
```

```python
import jax
import jax.numpy as jnp
from jax import lax
from jax.experimental import pallas as pl
from jax.experimental.pallas import tpu as pltpu
from jax.sharding import PartitionSpec as P

HALO = 8
EARLY = 8
ONES = 16
STRIP = 32
F32 = jnp.float32
BF16 = jnp.bfloat16
ALONG_X = (0, 1, 2, 3, 4)
ALONG_Y = (0, 3, 2, 1, 4)
VMEM = pl.BlockSpec(memory_space=pltpu.VMEM)


def iota(shape, dim):
    return lax.broadcasted_iota(jnp.int32, shape, dim)


def sides(fields, mask, got_in, got_out):
    chans = fields.shape[0] + 1
    odd = lax.rem(lax.axis_index("gx"), 2)
    west, own, east = [], [], []
    for c in range(chans):
        near = got_in[1 - odd, c]
        far = got_out[odd, c]
        near_low, near_high = near[:HALO].astype(F32), near[HALO:].astype(F32)
        far_low, far_high = far[:HALO].astype(F32), far[HALO:].astype(F32)
        west.append(jnp.where(odd == 1, near_high, far_high))
        east.append(jnp.where(odd == 1, far_low, near_low))
        own.append(fields[c].astype(F32) if c < chans - 1 else mask[...].astype(F32))
    return west, own, east


def edge_kernel(fields, mask, metric, biases, edges, halved, own_biases):
    feeds, span_x, _ = fields.shape
    for part, start in enumerate((0, span_x - HALO)):
        rows = slice(part * HALO, (part + 1) * HALO)
        edges[:feeds, rows] = fields[:, start : start + HALO].astype(BF16)
        edges[feeds, rows] = mask[start : start + HALO].astype(F32).astype(BF16)
    halved[...] = metric[...] * 0.5
    own_biases[...] = biases[...]


def pack_kernel(fields, mask, got_in, got_out, pay_in, pay_out, own_low, own_top):
    chans = fields.shape[0] + 1
    span_x, span_y = mask.shape
    wide = span_x + 2 * HALO
    lat, last = lax.axis_index("gy"), lax.axis_size("gy") - 1
    odd = lax.rem(lat, 2) == 1
    west, own, east = sides(fields, mask, got_in, got_out)
    pad = jnp.zeros((span_y - wide, span_y), F32)
    slot = 4 * HALO
    lane = iota((wide, span_y), 1)
    low, top = [], []
    for first in range(0, chans, span_y // slot):
        group = range(first, min(first + span_y // slot, chans))
        gathered = jnp.zeros((wide, span_y), F32)
        for i, c in enumerate(group):
            col = jnp.concatenate([west[c], own[c], east[c]], axis=0)
            here = (lane >= i * slot) & (lane < (i + 1) * slot)
            gathered = jnp.where(here, turn(col, i * slot + 2 * HALO), gathered)
        turned = jnp.concatenate([gathered, pad], axis=0).T
        for i, c in enumerate(group):
            own_top[c] = turned[i * slot : i * slot + 2 * HALO]
            own_low[c] = turned[i * slot + 2 * HALO : (i + 1) * slot]
            top.append(turned[i * slot + HALO : i * slot + 2 * HALO])
            low.append(turned[i * slot + 2 * HALO : i * slot + 3 * HALO])
    low = jnp.concatenate(low, axis=0)
    top = jnp.concatenate(top, axis=0)
    a, b = iota((span_y, span_y), 0), iota((span_y, span_y), 1)
    flip_x = (a + b == wide - 1).astype(BF16)
    a, b = iota((chans * HALO, chans * HALO), 0), iota((chans * HALO, chans * HALO), 1)
    flip_y = ((a // HALO == b // HALO) & (a % HALO + b % HALO == HALO - 1)).astype(BF16)
    mirrored = jnp.dot(top.astype(BF16), flip_x, preferred_element_type=F32).astype(BF16)
    mirrored = jnp.dot(flip_y, mirrored, preferred_element_type=F32)
    out_top = jnp.where(lat == last, mirrored, top)
    for c in range(chans):
        part = slice(c * HALO, (c + 1) * HALO)
        pay_in[c] = jnp.where(odd, low[part], top[part]).astype(BF16)
        pay_out[c] = jnp.where(odd, out_top[part], low[part]).astype(BF16)


def ones_rows(lanes):
    return (iota((ONES, lanes), 0) < 3).astype(BF16)


def turn(v, by):
    return pltpu.roll(v, by % v.shape[-1], v.ndim - 1)


def first_taps(window, order):
    pieces = [[] for _ in range(5)]
    for w in window:
        west, here, east = w[:8], w[1:9], w[2:]
        pieces[0].append(turn(west, 1) + turn(east, -1))
        pieces[1].append(west + east)
        pieces[2].append(turn(west, -1) + turn(east, 1))
        pieces[3].append(turn(here, 1) + turn(here, -1))
        pieces[4].append(here)
    stacked = jnp.concatenate([p for t in order for p in pieces[t]], axis=0).astype(BF16)
    return jnp.concatenate([stacked, ones_rows(stacked.shape[1])], axis=0)


def hidden_taps(load, row, order):
    parts = [
        load(1, row - 1) + load(2, row + 1),
        load(0, row - 1) + load(0, row + 1),
        load(2, row - 1) + load(1, row + 1),
        load(1, row) + load(2, row),
        load(0, row),
    ]
    return jnp.concatenate([parts[t] for t in order] + [ones_rows(parts[0].shape[1])], axis=0)


def loader(src):
    seen = {}

    def load(version, row):
        if (version, row) not in seen:
            seen[version, row] = src[version, row]
        return seen[version, row]

    return load


def activate(summed, ocean_row):
    ocean = jnp.broadcast_to(ocean_row, (16, ocean_row.shape[1])).astype(BF16)
    ocean = jnp.concatenate([ocean] * (summed.shape[0] // 16), axis=0)
    return jnp.maximum(summed.astype(BF16), jnp.zeros((), BF16)) * ocean


def put(dst, row, v):
    dst[0, row] = v
    dst[1, row] = turn(v, 1)
    dst[2, row] = turn(v, -1)


def bias_columns(biases, k):
    hid = biases.shape[1]
    a, b = iota((hid, hid), 0), iota((hid, hid), 1)
    row = jnp.broadcast_to(biases[k : k + 1, :], (hid, hid))
    rest = jnp.sum(jnp.where(a == b, row, 0.0), axis=1, keepdims=True)
    spread = jnp.zeros((hid, ONES), F32)
    at = iota((hid, ONES), 1)
    for i in range(3):
        piece = rest.astype(BF16).astype(F32)
        spread = jnp.where(at == i, jnp.broadcast_to(piece, (hid, ONES)), spread)
        rest = rest - piece
    return spread


def arrange_weights(w_first, w_mid, w_last, biases, big, hidden, final):
    taps, feeds, hid = w_first.shape
    n_mid = w_mid.shape[0]
    depth = taps * feeds * 8
    final[...] = jnp.zeros_like(final)
    lanes = 128
    stacked = [w_first[t].astype(F32) for t in range(taps)]
    stacked = jnp.concatenate(stacked + [jnp.zeros((lanes - taps * feeds, hid), F32)], axis=0)
    stacked = jnp.concatenate([stacked, jnp.zeros((lanes, lanes - hid), F32)], axis=1).T
    a, b = iota((lanes, depth), 0), iota((lanes, depth), 1)
    place = (b // 8 == a).astype(BF16)
    spread = jnp.dot(stacked[:hid].astype(BF16), place, preferred_element_type=F32)
    for t in range(taps):
        final[: w_last.shape[1], t * hid : (t + 1) * hid] = w_last[t]
        for k in range(n_mid):
            hidden[k, :, t * hid : (t + 1) * hid] = w_mid[k, t]
    sub = iota((hid, depth), 1) % 8
    first_bias = bias_columns(biases, 0).astype(BF16)
    for r in range(8):
        big[r * hid : (r + 1) * hid, :depth] = jnp.where(sub == r, spread, 0.0).astype(BF16)
        big[r * hid : (r + 1) * hid, depth:] = first_bias
    for k in range(n_mid):
        hidden[k, :, taps * hid :] = bias_columns(biases, k + 1).astype(BF16)


def waits_long():
    place = lax.rem(lax.axis_index("gx"), lax.axis_size("gx") // 4)
    top = lax.axis_index("gy") == lax.axis_size("gy") - 1
    origin = (lax.axis_index("gx") == 0) & (lax.axis_index("gy") == 0)
    return jnp.logical_not(origin) & ((place == 0) | (top & (place < EARLY)))


def halves(v):
    half = v.shape[1] // 2
    return v[:, :half], v[:, half:]


def masked_stress(summed, ocean_row):
    return (summed[:8] * ocean_row).astype(BF16).astype(F32)


def inner_columns(fields, mask, w_first, w_mid, w_last, biases, stress, kept, big, hidden, final, ext, h_a, h_b):
    feeds, span_x, span_y = fields.shape
    n_mid = w_mid.shape[0]
    hid = w_first.shape[2]
    arrange_weights(w_first, w_mid, w_last, biases, big, hidden, final)
    for c in range(feeds):
        ext[c, :HALO] = jnp.zeros((HALO, span_y), F32)
        ext[c, HALO : HALO + span_x] = fields[c].astype(F32)
        ext[c, HALO + span_x :] = jnp.zeros((HALO, span_y), F32)
    ext[feeds, HALO : HALO + span_x] = mask[...].astype(F32)

    def ocean_row(row):
        return ext[feeds, HALO + row : HALO + row + 1, :]

    def keep(k, row, v):
        for slot, at in enumerate((k, k + 1, span_x - k - 2, span_x - k - 1)):
            if row == at:
                kept[k - 1, slot] = v

    for start in range(0, span_x, 16):
        taps = [
            first_taps([ext[c, HALO + row - 1 : HALO + row + 9, :] for c in range(feeds)], ALONG_X)
            for row in (start, start + 8)
        ]
        summed = jnp.dot(big[...], jnp.concatenate(taps, axis=1), preferred_element_type=F32)
        for part, row in zip(halves(summed), (start, start + 8)):
            for r in range(8):
                v = activate(part[r * hid : (r + 1) * hid], ocean_row(row + r))
                put(h_a, row + r, v)
                keep(1, row + r, v)

    def layer(weights, src, k, finish):
        cached = loader(src)
        for start in range(k, span_x - k, 2):
            taps = [hidden_taps(cached, row, ALONG_X) for row in (start, start + 1)]
            summed = jnp.dot(weights, jnp.concatenate(taps, axis=1), preferred_element_type=F32)
            for part, row in zip(halves(summed), (start, start + 1)):
                finish(part, row)

    src, dst = h_a, h_b
    for k in range(2, n_mid + 2):

        def finish(summed, row):
            v = activate(summed, ocean_row(row))
            put(dst, row, v)
            keep(k, row, v)

        layer(hidden[k - 2], src, k, finish)
        src, dst = dst, src

    def finish(summed, row):
        v = masked_stress(summed, ocean_row(row))
        for c in range(3):
            stress[c, HALO + row : HALO + row + 1, :] = v[c : c + 1]

    layer(final[...], src, n_mid + 2, finish)


def early_kernel(
    edges, got_in, fields, mask, w_first, w_mid, w_last, biases,
    edges_out, stress, kept, big, hidden, final, ext, h_a, h_b,
):
    del got_in
    edges_out[...] = edges[...]

    @pl.when(waits_long())
    def _():
        inner_columns(
            fields, mask, w_first, w_mid, w_last, biases, stress, kept, big, hidden, final, ext, h_a, h_b
        )


def late_kernel(
    fields, mask, w_first, w_mid, w_last, biases, stress_in, kept_in, big_in, hidden_in, final_in, lat_out,
    stress, kept, big, hidden, final, ext, h_a, h_b,
):
    del lat_out

    @pl.when(waits_long())
    def _():
        pairs = ((stress_in, stress), (kept_in, kept), (big_in, big), (hidden_in, hidden), (final_in, final))
        for done, here in pairs:
            here[...] = done[...]

    @pl.when(jnp.logical_not(waits_long()))
    def _():
        inner_columns(
            fields, mask, w_first, w_mid, w_last, biases, stress, kept, big, hidden, final, ext, h_a, h_b
        )


def side_layers(ext, kept, span_x, big, hidden, final, src, dst, stress):
    n_mid, hid, _ = hidden.shape
    feeds = ext.shape[0] - 1
    starts = (-6, span_x - 2)

    def places(k, slot):
        return k - 8 + slot, span_x - 2 - k + slot

    def ocean_row(row):
        return ext[feeds, HALO + row : HALO + row + 1, :]

    def fill(dst, k):
        for slot in range(2):
            put(dst.at[0], 8 + slot, kept[k - 1, slot])
            put(dst.at[1], slot, kept[k - 1, 2 + slot])

    taps = [
        first_taps([ext[c, HALO + row - 1 : HALO + row + 9, :] for c in range(feeds)], ALONG_X) for row in starts
    ]
    summed = jnp.dot(big[...], jnp.concatenate(taps, axis=1), preferred_element_type=F32)
    for side, part in enumerate(halves(summed)):
        for slot in range(2, 8):
            row = places(1, slot)[side]
            r = row - starts[side]
            put(src.at[side], slot, activate(part[r * hid : (r + 1) * hid], ocean_row(row)))
    fill(src, 1)
    yield
    for k in range(2, n_mid + 3):
        loads = [loader(src.at[side]) for side in range(2)]
        weights = hidden[k - 2] if k < n_mid + 2 else final[...]
        for slot in range(2, 8):
            taps = [hidden_taps(loads[0], slot + 1, ALONG_X), hidden_taps(loads[1], slot - 1, ALONG_X)]
            summed = jnp.dot(weights, jnp.concatenate(taps, axis=1), preferred_element_type=F32)
            for side, part in enumerate(halves(summed)):
                row = places(k, slot)[side]
                if k < n_mid + 2:
                    put(dst.at[side], slot, activate(part, ocean_row(row)))
                else:
                    v = masked_stress(part, ocean_row(row))
                    for c in range(3):
                        stress[c, HALO + row : HALO + row + 1, :] = v[c : c + 1]
        yield
        if k < n_mid + 2:
            fill(dst, k)
        src, dst = dst, src


def strip_layers(ext, span_y, big, hidden, final, src, dst, edge):
    n_mid, hid, _ = hidden.shape
    feeds = ext.shape[0] - 1

    def ocean_row(row):
        return ext[feeds, row : row + 1, :]

    def put_both(dst, row, v):
        for half in range(2):
            lanes = slice(half * span_y, (half + 1) * span_y)
            part = v[:, lanes]
            dst[0, row, :, lanes] = part
            dst[1, row, :, lanes] = turn(part, 1)
            dst[2, row, :, lanes] = turn(part, -1)

    for row in (8, 16):
        taps = [
            first_taps([ext[c, row - 1 : row + 9, half * span_y : (half + 1) * span_y] for c in range(feeds)], ALONG_Y)
            for half in range(2)
        ]
        summed = jnp.dot(big[...], jnp.concatenate(taps, axis=1), preferred_element_type=F32)
        for r in range(8):
            put_both(src, row + r, activate(summed[r * hid : (r + 1) * hid], ocean_row(row + r)))
        yield
    for k in range(n_mid):
        cached = loader(src)
        for row in range(10 + k, 22 - k):
            taps = hidden_taps(cached, row, ALONG_Y)
            summed = jnp.dot(hidden[k], taps, preferred_element_type=F32)
            put_both(dst, row, activate(summed, ocean_row(row)))
        yield
        src, dst = dst, src
    slot = 2 * HALO
    cached = loader(src)
    for row in range(13, 19):
        summed = jnp.dot(final[...], hidden_taps(cached, row, ALONG_Y), preferred_element_type=F32)
        v = masked_stress(summed, ocean_row(row))
        for c in range(3):
            edge[c * slot + row - 13 : c * slot + row - 12, :] = v[c : c + 1, :span_y]
            edge[c * slot + row - 5 : c * slot + row - 4, :] = v[c : c + 1, span_y:]
        if row % 2:
            yield


def edge_lines_kernel(
    fields, mask, got_in, got_out, own_low, own_top, lat_in, lat_out, stress_in, kept, big, hidden, final, halved, out,
    ext, ext_strip, rows_a, rows_b, h_a, h_b, stress, edge,
):
    feeds, span_x, span_y = fields.shape
    lat, last = lax.axis_index("gy"), lax.axis_size("gy") - 1
    odd = lax.rem(lat, 2) == 1
    lower = lax.axis_index("gx") < lax.axis_size("gx") // 2
    partner = jnp.where(jnp.where(lat == last, lower, odd), 1, 0)
    stress[...] = stress_in[...]
    west, own, east = sides(fields, mask, got_in, got_out)
    for c in range(feeds + 1):
        ext[c, :HALO] = west[c]
        ext[c, HALO : HALO + span_x] = own[c]
        ext[c, HALO + span_x :] = east[c]
    for c in range(feeds + 1):
        inner = lat_in[c].astype(F32)
        outer = lat_out[partner, c].astype(F32)
        outer = jnp.where(lat == 0, jnp.zeros_like(outer), outer)
        below = jnp.where(odd, inner, outer)
        above = jnp.where(odd, outer, inner)
        ext_strip[c, 6:14, :span_y] = below
        ext_strip[c, 14:30, :span_y] = own_low[c]
        ext_strip[c, 2:18, span_y:] = own_top[c]
        ext_strip[c, 18:26, span_y:] = above

    todo = [
        strip_layers(ext_strip, span_y, big, hidden, final, h_a, h_b, edge),
        side_layers(ext, kept, span_x, big, hidden, final, rows_a, rows_b, stress),
    ]
    while todo:
        todo = [layers for layers in todo if next(layers, todo) is None]

    slot = 2 * HALO
    turned = edge[...].T[HALO - 1 : HALO + span_x + 1]

    half_x = halved[0:1, :]
    half_y = halved[1:2, :]
    ocean = mask[...].astype(F32)
    lane = iota((span_x + 2, span_y), 1)
    inner = lane[:span_x]
    planes, north, south = [], [], []
    for c in range(3):
        low = turn(turned, -(c * slot + 1))
        high = turn(turned, span_y - 5 - (c * slot + HALO))
        plane = jnp.where(lane < 5, low, jnp.where(lane >= span_y - 5, high, stress[c, HALO - 1 : HALO + span_x + 1, :]))
        here = plane[1 : 1 + span_x]
        beyond = turn(turned[1 : 1 + span_x], span_y - 1 - (c * slot + HALO + 5))
        below = turn(turned[1 : 1 + span_x], -c * slot)
        planes.append(plane)
        north.append(jnp.where(inner == span_y - 1, beyond, turn(here, -1)))
        south.append(jnp.where(inner == 0, below, turn(here, 1)))

    def diff_x(c):
        return (planes[c][2:] - planes[c][:span_x]) * half_x

    def diff_y(c):
        return (north[c] - south[c]) * half_y

    out[0] = (diff_x(0) + diff_y(1)) * ocean
    out[1] = (diff_x(1) + diff_y(2)) * ocean


def pack(fields, mask, got_in, got_out):
    chans, span_y = fields.shape[0] + 1, mask.shape[1]
    return pl.pallas_call(
        pack_kernel,
        out_shape=[jax.ShapeDtypeStruct((chans, HALO, span_y), BF16)] * 2
        + [jax.ShapeDtypeStruct((chans, 2 * HALO, span_y), F32)] * 2,
        in_specs=[VMEM] * 4,
        out_specs=[VMEM] * 4,
        compiler_params=pltpu.CompilerParams(vmem_limit_bytes=4 * 1024 * 1024),
        name="pack_rows",
    )(fields, mask, got_in, got_out)


def outermost(fields, mask, metric, biases):
    feeds, span_x, span_y = fields.shape
    return pl.pallas_call(
        edge_kernel,
        out_shape=[
            jax.ShapeDtypeStruct((feeds + 1, 2 * HALO, span_y), BF16),
            jax.ShapeDtypeStruct(metric.shape, F32),
            jax.ShapeDtypeStruct(biases.shape, F32),
        ],
        in_specs=[VMEM] * 4,
        out_specs=[VMEM] * 3,
        compiler_params=pltpu.CompilerParams(vmem_limit_bytes=4 * 1024 * 1024),
        cost_estimate=pl.CostEstimate(flops=10_000_000_000, bytes_accessed=1_000_000, transcendentals=0),
        name="outermost_columns",
    )(fields, mask, metric, biases)


def hold_kernel(edges, edges_out):
    edges_out[...] = edges[...]


def hold(edges):
    return pl.pallas_call(
        hold_kernel,
        out_shape=jax.ShapeDtypeStruct(edges.shape, edges.dtype),
        in_specs=[VMEM],
        out_specs=VMEM,
        compiler_params=pltpu.CompilerParams(vmem_limit_bytes=4 * 1024 * 1024),
        cost_estimate=pl.CostEstimate(flops=10_000_000_000, bytes_accessed=1_000_000, transcendentals=0),
        name="hold",
    )(edges)


def inner_shapes(fields, w_first, w_mid):
    feeds, span_x, span_y = fields.shape
    taps, _, hid = w_first.shape
    n_mid = w_mid.shape[0]
    rows = span_x + 2 * HALO
    outs = [
        jax.ShapeDtypeStruct((3, rows, span_y), F32),
        jax.ShapeDtypeStruct((n_mid + 1, 4, hid, span_y), BF16),
        jax.ShapeDtypeStruct((8 * hid, taps * feeds * 8 + ONES), BF16),
        jax.ShapeDtypeStruct((n_mid, hid, taps * hid + ONES), BF16),
        jax.ShapeDtypeStruct((16, taps * hid + ONES), BF16),
    ]
    scratch = [
        pltpu.VMEM((feeds + 1, rows, span_y), F32),
        pltpu.VMEM((3, span_x, hid, span_y), BF16),
        pltpu.VMEM((3, span_x, hid, span_y), BF16),
    ]
    return outs, scratch


def early(edges, got_in, fields, mask, w_first, w_mid, w_last, biases):
    outs, scratch = inner_shapes(fields, w_first, w_mid)
    return pl.pallas_call(
        early_kernel,
        out_shape=[jax.ShapeDtypeStruct(edges.shape, edges.dtype)] + outs,
        in_specs=[VMEM] * 8,
        out_specs=[VMEM] * 6,
        scratch_shapes=scratch,
        compiler_params=pltpu.CompilerParams(vmem_limit_bytes=12 * 1024 * 1024),
        name="inner_early",
    )(edges, got_in, fields, mask, w_first, w_mid, w_last, biases)


def late(fields, mask, w_first, w_mid, w_last, biases, done, lat_out):
    outs, scratch = inner_shapes(fields, w_first, w_mid)
    return pl.pallas_call(
        late_kernel,
        out_shape=outs,
        in_specs=[VMEM] * 12,
        out_specs=[VMEM] * 5,
        scratch_shapes=scratch,
        compiler_params=pltpu.CompilerParams(vmem_limit_bytes=12 * 1024 * 1024),
        cost_estimate=pl.CostEstimate(flops=5_000_000_000, bytes_accessed=20_000_000, transcendentals=0),
        name="inner_late",
    )(fields, mask, w_first, w_mid, w_last, biases, *done, lat_out)


def edge_lines(fields, mask, got_in, got_out, own_low, own_top, lat_in, lat_out, inner, halved):
    feeds, span_x, span_y = fields.shape
    stress, _, _, hidden, _ = inner
    hid = hidden.shape[1]
    return pl.pallas_call(
        edge_lines_kernel,
        out_shape=jax.ShapeDtypeStruct((2, span_x, span_y), F32),
        in_specs=[VMEM] * 14,
        out_specs=VMEM,
        scratch_shapes=[
            pltpu.VMEM((feeds + 1, span_x + 2 * HALO, span_y), F32),
            pltpu.VMEM((feeds + 1, STRIP, 2 * span_y), F32),
            pltpu.VMEM((2, 3, 10, hid, span_y), BF16),
            pltpu.VMEM((2, 3, 10, hid, span_y), BF16),
            pltpu.VMEM((3, STRIP, hid, 2 * span_y), BF16),
            pltpu.VMEM((3, STRIP, hid, 2 * span_y), BF16),
            pltpu.VMEM(stress.shape, F32),
            pltpu.VMEM((span_y, span_y), F32),
        ],
        compiler_params=pltpu.CompilerParams(vmem_limit_bytes=12 * 1024 * 1024),
        name="edge_lines",
    )(fields, mask, got_in, got_out, own_low, own_top, lat_in, lat_out, *inner, halved)


def latitude_swaps(count_x, count_y):
    at = lambda g, y: g * count_y + y
    up = [(at(g, y), at(g, y + 1)) for g in range(count_x) for y in range(0, count_y, 2)]
    return up + [(target, source) for source, target in up]


def latitude_groups(count_x, count_y):
    at = lambda g, y: g * count_y + y
    pairs = [[at(g, y), at(g, y + 1)] for g in range(count_x) for y in range(1, count_y - 1, 2)]
    pairs += [[at(g, count_y - 1), at(count_x - 1 - g, count_y - 1)] for g in range(count_x // 2)]
    return pairs + [[at(g, 0), at((g + 1) % count_x, 0)] for g in range(1, count_x, 2)]


def on_device(fields, ocean_mask, metric, w_first, w_mid, w_last, biases):
    count_x, count_y = lax.axis_size("gx"), lax.axis_size("gy")
    inside = [[i, i + 1] for i in range(0, count_x, 2)]
    across = [[i, (i + 1) % count_x] for i in range(1, count_x, 2)]
    fields = fields.astype(F32)
    edges, halved, biases = outermost(fields, ocean_mask, metric, biases)
    weights = (jnp.swapaxes(w_first, 1, 2), w_mid, w_last, biases)
    edges = hold(hold(edges))
    got_in = lax.all_gather(edges, "gx", axis_index_groups=inside)
    edges, *done = early(edges, got_in, fields, ocean_mask, *weights)
    got_out = lax.all_gather(edges, "gx", axis_index_groups=across)
    pay_in, pay_out, own_low, own_top = pack(fields, ocean_mask, got_in, got_out)
    lat_in = lax.ppermute(pay_in, ("gx", "gy"), latitude_swaps(count_x, count_y))
    lat_out = lax.all_gather(pay_out, ("gx", "gy"), axis_index_groups=latitude_groups(count_x, count_y))
    inner = late(fields, ocean_mask, *weights, done, lat_out)
    return edge_lines(fields, ocean_mask, got_in, got_out, own_low, own_top, lat_in, lat_out, inner, halved)


def solution(mesh):
    placed = (P(None, "gx", "gy"), P("gx", "gy"), P(None, "gy"), P(), P(), P(), P())
    return jax.shard_map(
        on_device, mesh=mesh, in_specs=placed, out_specs=P(None, "gx", "gy"), check_vma=False
    )
```

```python
import jax
import jax.numpy as jnp
from jax import lax
from jax.experimental import pallas as pl
from jax.experimental.pallas import tpu as pltpu
from jax.sharding import PartitionSpec as P

HALO = 8
EARLY = 8
ONES = 16
STRIP = 32
F32 = jnp.float32
BF16 = jnp.bfloat16
ALONG_X = (0, 1, 2, 3, 4)
ALONG_Y = (0, 3, 2, 1, 4)
VMEM = pl.BlockSpec(memory_space=pltpu.VMEM)


def iota(shape, dim):
    return lax.broadcasted_iota(jnp.int32, shape, dim)


def sides(fields, mask, got_in, got_out):
    chans = fields.shape[0] + 1
    odd = lax.rem(lax.axis_index("gx"), 2)
    west, own, east = [], [], []
    for c in range(chans):
        near = got_in[1 - odd, c].astype(F32)
        far = got_out[odd, c].astype(F32)
        west.append(jnp.where(odd == 1, near, far))
        east.append(jnp.where(odd == 1, far, near))
        own.append(fields[c].astype(F32) if c < chans - 1 else mask[...].astype(F32))
    return west, own, east


def edge_kernel(columns, mask, metric, edges_in, edges_out, halved):
    feeds = columns.shape[0]
    span_x = mask.shape[0]
    odd = lax.rem(lax.axis_index("gx"), 2) == 1
    for c in range(feeds + 1):
        if c < feeds:
            low, high = columns[c, :HALO].astype(F32), columns[c, HALO:].astype(F32)
        else:
            low, high = mask[:HALO].astype(F32), mask[span_x - HALO :].astype(F32)
        edges_in[c] = jnp.where(odd, low, high).astype(BF16)
        edges_out[c] = jnp.where(odd, high, low).astype(BF16)
    halved[...] = metric[...] * 0.5


def pack_kernel(fields, mask, got_in, got_out, pay_in, pay_out, own_low, own_top):
    chans = fields.shape[0] + 1
    span_x, span_y = mask.shape
    wide = span_x + 2 * HALO
    lat, last = lax.axis_index("gy"), lax.axis_size("gy") - 1
    odd = lax.rem(lat, 2) == 1
    west, own, east = sides(fields, mask, got_in, got_out)
    pad = jnp.zeros((span_y - wide, span_y), F32)
    slot = 4 * HALO
    lane = iota((wide, span_y), 1)
    low, top = [], []
    for first in range(0, chans, span_y // slot):
        group = range(first, min(first + span_y // slot, chans))
        gathered = jnp.zeros((wide, span_y), F32)
        for i, c in enumerate(group):
            col = jnp.concatenate([west[c], own[c], east[c]], axis=0)
            here = (lane >= i * slot) & (lane < (i + 1) * slot)
            gathered = jnp.where(here, turn(col, i * slot + 2 * HALO), gathered)
        turned = jnp.concatenate([gathered, pad], axis=0).T
        for i, c in enumerate(group):
            own_top[c] = turned[i * slot : i * slot + 2 * HALO]
            own_low[c] = turned[i * slot + 2 * HALO : (i + 1) * slot]
            top.append(turned[i * slot + HALO : i * slot + 2 * HALO])
            low.append(turned[i * slot + 2 * HALO : i * slot + 3 * HALO])
    low = jnp.concatenate(low, axis=0)
    top = jnp.concatenate(top, axis=0)
    a, b = iota((span_y, span_y), 0), iota((span_y, span_y), 1)
    flip_x = (a + b == wide - 1).astype(BF16)
    a, b = iota((chans * HALO, chans * HALO), 0), iota((chans * HALO, chans * HALO), 1)
    flip_y = ((a // HALO == b // HALO) & (a % HALO + b % HALO == HALO - 1)).astype(BF16)
    mirrored = jnp.dot(top.astype(BF16), flip_x, preferred_element_type=F32).astype(BF16)
    mirrored = jnp.dot(flip_y, mirrored, preferred_element_type=F32)
    out_top = jnp.where(lat == last, mirrored, top)
    for c in range(chans):
        part = slice(c * HALO, (c + 1) * HALO)
        pay_in[c] = jnp.where(odd, low[part], top[part]).astype(BF16)
        pay_out[c] = jnp.where(odd, out_top[part], low[part]).astype(BF16)


def ones_rows(lanes):
    return (iota((ONES, lanes), 0) < 3).astype(BF16)


def turn(v, by):
    return pltpu.roll(v, by % v.shape[-1], v.ndim - 1)


def first_taps(window, order):
    pieces = [[] for _ in range(5)]
    for w in window:
        west, here, east = w[:8], w[1:9], w[2:]
        pieces[0].append(turn(west, 1) + turn(east, -1))
        pieces[1].append(west + east)
        pieces[2].append(turn(west, -1) + turn(east, 1))
        pieces[3].append(turn(here, 1) + turn(here, -1))
        pieces[4].append(here)
    stacked = jnp.concatenate([p for t in order for p in pieces[t]], axis=0).astype(BF16)
    return jnp.concatenate([stacked, ones_rows(stacked.shape[1])], axis=0)


def hidden_taps(load, row, order):
    parts = [
        load(1, row - 1) + load(2, row + 1),
        load(0, row - 1) + load(0, row + 1),
        load(2, row - 1) + load(1, row + 1),
        load(1, row) + load(2, row),
        load(0, row),
    ]
    return jnp.concatenate([parts[t] for t in order] + [ones_rows(parts[0].shape[1])], axis=0)


def loader(src):
    seen = {}

    def load(version, row):
        if (version, row) not in seen:
            seen[version, row] = src[version, row]
        return seen[version, row]

    return load


def activate(summed, ocean_row):
    ocean = jnp.broadcast_to(ocean_row, (16, ocean_row.shape[1])).astype(BF16)
    ocean = jnp.concatenate([ocean] * (summed.shape[0] // 16), axis=0)
    return jnp.maximum(summed.astype(BF16), jnp.zeros((), BF16)) * ocean


def put(dst, row, v):
    dst[0, row] = v
    dst[1, row] = turn(v, 1)
    dst[2, row] = turn(v, -1)


def bias_columns(biases, k):
    hid = biases.shape[1]
    a, b = iota((hid, hid), 0), iota((hid, hid), 1)
    row = jnp.broadcast_to(biases[k : k + 1, :], (hid, hid))
    rest = jnp.sum(jnp.where(a == b, row, 0.0), axis=1, keepdims=True)
    spread = jnp.zeros((hid, ONES), F32)
    at = iota((hid, ONES), 1)
    for i in range(3):
        piece = rest.astype(BF16).astype(F32)
        spread = jnp.where(at == i, jnp.broadcast_to(piece, (hid, ONES)), spread)
        rest = rest - piece
    return spread


def arrange_weights(w_first, w_mid, w_last, biases, big, hidden, final):
    taps, feeds, hid = w_first.shape
    n_mid = w_mid.shape[0]
    depth = taps * feeds * 8
    final[...] = jnp.zeros_like(final)
    lanes = 128
    stacked = [w_first[t].astype(F32) for t in range(taps)]
    stacked = jnp.concatenate(stacked + [jnp.zeros((lanes - taps * feeds, hid), F32)], axis=0)
    stacked = jnp.concatenate([stacked, jnp.zeros((lanes, lanes - hid), F32)], axis=1).T
    a, b = iota((lanes, depth), 0), iota((lanes, depth), 1)
    place = (b // 8 == a).astype(BF16)
    spread = jnp.dot(stacked[:hid].astype(BF16), place, preferred_element_type=F32)
    for t in range(taps):
        final[: w_last.shape[1], t * hid : (t + 1) * hid] = w_last[t]
        for k in range(n_mid):
            hidden[k, :, t * hid : (t + 1) * hid] = w_mid[k, t]
    sub = iota((hid, depth), 1) % 8
    first_bias = bias_columns(biases, 0).astype(BF16)
    for r in range(8):
        big[r * hid : (r + 1) * hid, :depth] = jnp.where(sub == r, spread, 0.0).astype(BF16)
        big[r * hid : (r + 1) * hid, depth:] = first_bias
    for k in range(n_mid):
        hidden[k, :, taps * hid :] = bias_columns(biases, k + 1).astype(BF16)


def waits_long():
    place = lax.rem(lax.axis_index("gx"), lax.axis_size("gx") // 4)
    top = lax.axis_index("gy") == lax.axis_size("gy") - 1
    origin = (lax.axis_index("gx") == 0) & (lax.axis_index("gy") == 0)
    return jnp.logical_not(origin) & ((place == 0) | (top & (place < EARLY)))


def halves(v):
    half = v.shape[1] // 2
    return v[:, :half], v[:, half:]


def masked_stress(summed, ocean_row):
    return (summed[:8] * ocean_row).astype(BF16).astype(F32)


def inner_columns(fields, mask, w_first, w_mid, w_last, biases, stress, kept, big, hidden, final, ext, h_a, h_b):
    feeds, span_x, span_y = fields.shape
    n_mid = w_mid.shape[0]
    hid = w_first.shape[2]
    arrange_weights(w_first, w_mid, w_last, biases, big, hidden, final)
    for c in range(feeds):
        ext[c, :HALO] = jnp.zeros((HALO, span_y), F32)
        ext[c, HALO : HALO + span_x] = fields[c].astype(F32)
        ext[c, HALO + span_x :] = jnp.zeros((HALO, span_y), F32)
    ext[feeds, HALO : HALO + span_x] = mask[...].astype(F32)

    def ocean_row(row):
        return ext[feeds, HALO + row : HALO + row + 1, :]

    def keep(k, row, v):
        for slot, at in enumerate((k, k + 1, span_x - k - 2, span_x - k - 1)):
            if row == at:
                kept[k - 1, slot] = v

    for start in range(0, span_x, 16):
        taps = [
            first_taps([ext[c, HALO + row - 1 : HALO + row + 9, :] for c in range(feeds)], ALONG_X)
            for row in (start, start + 8)
        ]
        summed = jnp.dot(big[...], jnp.concatenate(taps, axis=1), preferred_element_type=F32)
        for part, row in zip(halves(summed), (start, start + 8)):
            for r in range(8):
                v = activate(part[r * hid : (r + 1) * hid], ocean_row(row + r))
                put(h_a, row + r, v)
                keep(1, row + r, v)

    def layer(weights, src, k, finish):
        cached = loader(src)
        for start in range(k, span_x - k, 2):
            taps = [hidden_taps(cached, row, ALONG_X) for row in (start, start + 1)]
            summed = jnp.dot(weights, jnp.concatenate(taps, axis=1), preferred_element_type=F32)
            for part, row in zip(halves(summed), (start, start + 1)):
                finish(part, row)

    src, dst = h_a, h_b
    for k in range(2, n_mid + 2):

        def finish(summed, row):
            v = activate(summed, ocean_row(row))
            put(dst, row, v)
            keep(k, row, v)

        layer(hidden[k - 2], src, k, finish)
        src, dst = dst, src

    def finish(summed, row):
        v = masked_stress(summed, ocean_row(row))
        for c in range(3):
            stress[c, HALO + row : HALO + row + 1, :] = v[c : c + 1]

    layer(final[...], src, n_mid + 2, finish)


def early_kernel(
    edges, got_in, fields, mask, w_first, w_mid, w_last, biases,
    edges_out, stress, kept, big, hidden, final, ext, h_a, h_b,
):
    del got_in
    edges_out[...] = edges[...]

    @pl.when(waits_long())
    def _():
        inner_columns(
            fields, mask, w_first, w_mid, w_last, biases, stress, kept, big, hidden, final, ext, h_a, h_b
        )


def late_kernel(
    fields, mask, w_first, w_mid, w_last, biases, stress_in, kept_in, big_in, hidden_in, final_in, lat_out,
    stress, kept, big, hidden, final, ext, h_a, h_b,
):
    del lat_out

    @pl.when(waits_long())
    def _():
        pairs = ((stress_in, stress), (kept_in, kept), (big_in, big), (hidden_in, hidden), (final_in, final))
        for done, here in pairs:
            here[...] = done[...]

    @pl.when(jnp.logical_not(waits_long()))
    def _():
        inner_columns(
            fields, mask, w_first, w_mid, w_last, biases, stress, kept, big, hidden, final, ext, h_a, h_b
        )


def side_layers(ext, kept, span_x, big, hidden, final, src, dst, stress):
    n_mid, hid, _ = hidden.shape
    feeds = ext.shape[0] - 1
    starts = (-6, span_x - 2)

    def places(k, slot):
        return k - 8 + slot, span_x - 2 - k + slot

    def ocean_row(row):
        return ext[feeds, HALO + row : HALO + row + 1, :]

    def fill(dst, k):
        for slot in range(2):
            put(dst.at[0], 8 + slot, kept[k - 1, slot])
            put(dst.at[1], slot, kept[k - 1, 2 + slot])

    taps = [
        first_taps([ext[c, HALO + row - 1 : HALO + row + 9, :] for c in range(feeds)], ALONG_X) for row in starts
    ]
    summed = jnp.dot(big[...], jnp.concatenate(taps, axis=1), preferred_element_type=F32)
    for side, part in enumerate(halves(summed)):
        for slot in range(2, 8):
            row = places(1, slot)[side]
            r = row - starts[side]
            put(src.at[side], slot, activate(part[r * hid : (r + 1) * hid], ocean_row(row)))
    fill(src, 1)
    yield
    for k in range(2, n_mid + 3):
        loads = [loader(src.at[side]) for side in range(2)]
        weights = hidden[k - 2] if k < n_mid + 2 else final[...]
        for slot in range(2, 8):
            taps = [hidden_taps(loads[0], slot + 1, ALONG_X), hidden_taps(loads[1], slot - 1, ALONG_X)]
            summed = jnp.dot(weights, jnp.concatenate(taps, axis=1), preferred_element_type=F32)
            for side, part in enumerate(halves(summed)):
                row = places(k, slot)[side]
                if k < n_mid + 2:
                    put(dst.at[side], slot, activate(part, ocean_row(row)))
                else:
                    v = masked_stress(part, ocean_row(row))
                    for c in range(3):
                        stress[c, HALO + row : HALO + row + 1, :] = v[c : c + 1]
        yield
        if k < n_mid + 2:
            fill(dst, k)
        src, dst = dst, src


def strip_layers(ext, span_y, big, hidden, final, src, dst, edge):
    n_mid, hid, _ = hidden.shape
    feeds = ext.shape[0] - 1

    def ocean_row(row):
        return ext[feeds, row : row + 1, :]

    def put_both(dst, row, v):
        for half in range(2):
            lanes = slice(half * span_y, (half + 1) * span_y)
            part = v[:, lanes]
            dst[0, row, :, lanes] = part
            dst[1, row, :, lanes] = turn(part, 1)
            dst[2, row, :, lanes] = turn(part, -1)

    for row in (8, 16):
        taps = [
            first_taps([ext[c, row - 1 : row + 9, half * span_y : (half + 1) * span_y] for c in range(feeds)], ALONG_Y)
            for half in range(2)
        ]
        summed = jnp.dot(big[...], jnp.concatenate(taps, axis=1), preferred_element_type=F32)
        for r in range(8):
            put_both(src, row + r, activate(summed[r * hid : (r + 1) * hid], ocean_row(row + r)))
        yield
    for k in range(n_mid):
        cached = loader(src)
        for row in range(10 + k, 22 - k):
            taps = hidden_taps(cached, row, ALONG_Y)
            summed = jnp.dot(hidden[k], taps, preferred_element_type=F32)
            put_both(dst, row, activate(summed, ocean_row(row)))
        yield
        src, dst = dst, src
    slot = 2 * HALO
    cached = loader(src)
    for row in range(13, 19):
        summed = jnp.dot(final[...], hidden_taps(cached, row, ALONG_Y), preferred_element_type=F32)
        v = masked_stress(summed, ocean_row(row))
        for c in range(3):
            edge[c * slot + row - 13 : c * slot + row - 12, :] = v[c : c + 1, :span_y]
            edge[c * slot + row - 5 : c * slot + row - 4, :] = v[c : c + 1, span_y:]
        if row % 2:
            yield


def edge_lines_kernel(
    fields, mask, got_in, got_out, own_low, own_top, lat_in, lat_out, stress_in, kept, big, hidden, final, halved, out,
    ext, ext_strip, rows_a, rows_b, h_a, h_b, stress, edge,
):
    feeds, span_x, span_y = fields.shape
    lat, last = lax.axis_index("gy"), lax.axis_size("gy") - 1
    odd = lax.rem(lat, 2) == 1
    lower = lax.axis_index("gx") < lax.axis_size("gx") // 2
    partner = jnp.where(jnp.where(lat == last, lower, odd), 1, 0)
    stress[...] = stress_in[...]
    west, own, east = sides(fields, mask, got_in, got_out)
    for c in range(feeds + 1):
        ext[c, :HALO] = west[c]
        ext[c, HALO : HALO + span_x] = own[c]
        ext[c, HALO + span_x :] = east[c]
    for c in range(feeds + 1):
        inner = lat_in[c].astype(F32)
        outer = lat_out[partner, c].astype(F32)
        outer = jnp.where(lat == 0, jnp.zeros_like(outer), outer)
        below = jnp.where(odd, inner, outer)
        above = jnp.where(odd, outer, inner)
        ext_strip[c, 6:14, :span_y] = below
        ext_strip[c, 14:30, :span_y] = own_low[c]
        ext_strip[c, 2:18, span_y:] = own_top[c]
        ext_strip[c, 18:26, span_y:] = above

    todo = [
        strip_layers(ext_strip, span_y, big, hidden, final, h_a, h_b, edge),
        side_layers(ext, kept, span_x, big, hidden, final, rows_a, rows_b, stress),
    ]
    while todo:
        todo = [layers for layers in todo if next(layers, todo) is None]

    slot = 2 * HALO
    turned = edge[...].T[HALO - 1 : HALO + span_x + 1]

    half_x = halved[0:1, :]
    half_y = halved[1:2, :]
    ocean = mask[...].astype(F32)
    lane = iota((span_x + 2, span_y), 1)
    inner = lane[:span_x]
    planes, north, south = [], [], []
    for c in range(3):
        low = turn(turned, -(c * slot + 1))
        high = turn(turned, span_y - 5 - (c * slot + HALO))
        plane = jnp.where(lane < 5, low, jnp.where(lane >= span_y - 5, high, stress[c, HALO - 1 : HALO + span_x + 1, :]))
        here = plane[1 : 1 + span_x]
        beyond = turn(turned[1 : 1 + span_x], span_y - 1 - (c * slot + HALO + 5))
        below = turn(turned[1 : 1 + span_x], -c * slot)
        planes.append(plane)
        north.append(jnp.where(inner == span_y - 1, beyond, turn(here, -1)))
        south.append(jnp.where(inner == 0, below, turn(here, 1)))

    def diff_x(c):
        return (planes[c][2:] - planes[c][:span_x]) * half_x

    def diff_y(c):
        return (north[c] - south[c]) * half_y

    out[0] = (diff_x(0) + diff_y(1)) * ocean
    out[1] = (diff_x(1) + diff_y(2)) * ocean


def pack(fields, mask, got_in, got_out):
    chans, span_y = fields.shape[0] + 1, mask.shape[1]
    return pl.pallas_call(
        pack_kernel,
        out_shape=[jax.ShapeDtypeStruct((chans, HALO, span_y), BF16)] * 2
        + [jax.ShapeDtypeStruct((chans, 2 * HALO, span_y), F32)] * 2,
        in_specs=[VMEM] * 4,
        out_specs=[VMEM] * 4,
        compiler_params=pltpu.CompilerParams(vmem_limit_bytes=4 * 1024 * 1024),
        name="pack_rows",
    )(fields, mask, got_in, got_out)


def outermost(fields, mask, metric):
    feeds, span_x, span_y = fields.shape
    columns = jnp.concatenate([fields[:, :HALO], fields[:, span_x - HALO :]], axis=1)
    return pl.pallas_call(
        edge_kernel,
        out_shape=[
            jax.ShapeDtypeStruct((feeds + 1, HALO, span_y), BF16),
            jax.ShapeDtypeStruct((feeds + 1, HALO, span_y), BF16),
            jax.ShapeDtypeStruct(metric.shape, F32),
        ],
        in_specs=[VMEM] * 3,
        out_specs=[VMEM] * 3,
        compiler_params=pltpu.CompilerParams(vmem_limit_bytes=4 * 1024 * 1024),
        cost_estimate=pl.CostEstimate(flops=10_000_000_000, bytes_accessed=1_000_000, transcendentals=0),
        name="outermost_columns",
    )(columns, mask, metric)


def inner_shapes(fields, w_first, w_mid):
    feeds, span_x, span_y = fields.shape
    taps, _, hid = w_first.shape
    n_mid = w_mid.shape[0]
    rows = span_x + 2 * HALO
    outs = [
        jax.ShapeDtypeStruct((3, rows, span_y), F32),
        jax.ShapeDtypeStruct((n_mid + 1, 4, hid, span_y), BF16),
        jax.ShapeDtypeStruct((8 * hid, taps * feeds * 8 + ONES), BF16),
        jax.ShapeDtypeStruct((n_mid, hid, taps * hid + ONES), BF16),
        jax.ShapeDtypeStruct((16, taps * hid + ONES), BF16),
    ]
    scratch = [
        pltpu.VMEM((feeds + 1, rows, span_y), F32),
        pltpu.VMEM((3, span_x, hid, span_y), BF16),
        pltpu.VMEM((3, span_x, hid, span_y), BF16),
    ]
    return outs, scratch


def early(edges, got_in, fields, mask, w_first, w_mid, w_last, biases):
    outs, scratch = inner_shapes(fields, w_first, w_mid)
    return pl.pallas_call(
        early_kernel,
        out_shape=[jax.ShapeDtypeStruct(edges.shape, edges.dtype)] + outs,
        in_specs=[VMEM] * 8,
        out_specs=[VMEM] * 6,
        scratch_shapes=scratch,
        compiler_params=pltpu.CompilerParams(vmem_limit_bytes=12 * 1024 * 1024),
        name="inner_early",
    )(edges, got_in, fields, mask, w_first, w_mid, w_last, biases)


def late(fields, mask, w_first, w_mid, w_last, biases, done, lat_out):
    outs, scratch = inner_shapes(fields, w_first, w_mid)
    return pl.pallas_call(
        late_kernel,
        out_shape=outs,
        in_specs=[VMEM] * 12,
        out_specs=[VMEM] * 5,
        scratch_shapes=scratch,
        compiler_params=pltpu.CompilerParams(vmem_limit_bytes=12 * 1024 * 1024),
        cost_estimate=pl.CostEstimate(flops=5_000_000_000, bytes_accessed=20_000_000, transcendentals=0),
        name="inner_late",
    )(fields, mask, w_first, w_mid, w_last, biases, *done, lat_out)


def edge_lines(fields, mask, got_in, got_out, own_low, own_top, lat_in, lat_out, inner, halved):
    feeds, span_x, span_y = fields.shape
    stress, _, _, hidden, _ = inner
    hid = hidden.shape[1]
    return pl.pallas_call(
        edge_lines_kernel,
        out_shape=jax.ShapeDtypeStruct((2, span_x, span_y), F32),
        in_specs=[VMEM] * 14,
        out_specs=VMEM,
        scratch_shapes=[
            pltpu.VMEM((feeds + 1, span_x + 2 * HALO, span_y), F32),
            pltpu.VMEM((feeds + 1, STRIP, 2 * span_y), F32),
            pltpu.VMEM((2, 3, 10, hid, span_y), BF16),
            pltpu.VMEM((2, 3, 10, hid, span_y), BF16),
            pltpu.VMEM((3, STRIP, hid, 2 * span_y), BF16),
            pltpu.VMEM((3, STRIP, hid, 2 * span_y), BF16),
            pltpu.VMEM(stress.shape, F32),
            pltpu.VMEM((span_y, span_y), F32),
        ],
        compiler_params=pltpu.CompilerParams(vmem_limit_bytes=12 * 1024 * 1024),
        name="edge_lines",
    )(fields, mask, got_in, got_out, own_low, own_top, lat_in, lat_out, *inner, halved)


def latitude_swaps(count_x, count_y):
    at = lambda g, y: g * count_y + y
    up = [(at(g, y), at(g, y + 1)) for g in range(count_x) for y in range(0, count_y, 2)]
    return up + [(target, source) for source, target in up]


def latitude_groups(count_x, count_y):
    at = lambda g, y: g * count_y + y
    pairs = [[at(g, y), at(g, y + 1)] for g in range(count_x) for y in range(1, count_y - 1, 2)]
    pairs += [[at(g, count_y - 1), at(count_x - 1 - g, count_y - 1)] for g in range(count_x // 2)]
    return pairs + [[at(g, 0), at((g + 1) % count_x, 0)] for g in range(1, count_x, 2)]


def on_device(fields, ocean_mask, metric, w_first, w_mid, w_last, biases):
    count_x, count_y = lax.axis_size("gx"), lax.axis_size("gy")
    inside = [[i, i + 1] for i in range(0, count_x, 2)]
    across = [[i, (i + 1) % count_x] for i in range(1, count_x, 2)]
    weights = (jnp.swapaxes(w_first, 1, 2), w_mid, w_last, biases)
    edges_in, edges, halved = outermost(fields, ocean_mask, metric)
    got_in = lax.all_gather(edges_in, "gx", axis_index_groups=inside)
    edges, *done = early(edges, got_in, fields, ocean_mask, *weights)
    got_out = lax.all_gather(edges, "gx", axis_index_groups=across)
    pay_in, pay_out, own_low, own_top = pack(fields, ocean_mask, got_in, got_out)
    lat_in = lax.ppermute(pay_in, ("gx", "gy"), latitude_swaps(count_x, count_y))
    lat_out = lax.all_gather(pay_out, ("gx", "gy"), axis_index_groups=latitude_groups(count_x, count_y))
    inner = late(fields, ocean_mask, *weights, done, lat_out)
    return edge_lines(fields, ocean_mask, got_in, got_out, own_low, own_top, lat_in, lat_out, inner, halved)


def solution(mesh):
    placed = (P(None, "gx", "gy"), P("gx", "gy"), P(None, "gy"), P(), P(), P(), P())
    return jax.shard_map(
        on_device, mesh=mesh, in_specs=placed, out_specs=P(None, "gx", "gy"), check_vma=False
    )
```
